256 devices in a mesh: ctx: 64 (over y, z, core), head: 4 (over x).
Axes of the slice: x: 4, y: 4, z: 8, core: 2. Of those that a mesh axis runs over, the one named last changes fastest.
Arguments:
- queries: bfloat16 [24576, 6144], P(('ctx', 'head')), may hold values from -9 to 9
- keys: bfloat16 [24576, 6144], P(('ctx', 'head')), may hold values from -9 to 9
- values: bfloat16 [24576, 6144], P(('ctx', 'head')), may hold values from -6 to 6
- grad_out: bfloat16 [24576, 6144], P(('ctx', 'head')), may hold values from -6 to 6
- segment: int32 [24576], P('ctx'), may hold values from 0 to 383, never falling along the last dimension, each value on 1 to 256 neighbouring positions
- lists: int32 [192, 2, 2], P('ctx'), may hold values from 0 to 192, as said below
Outputs:
- attended: bfloat16 [24576, 6144], P(('ctx', 'head'))
- grad_queries: bfloat16 [24576, 6144], P(('ctx', 'head'))
- grad_keys: bfloat16 [24576, 6144], P(('ctx', 'head'))
- grad_values: bfloat16 [24576, 6144], P(('ctx', 'head'))
The draws below stay inside these ranges and needn't reach their ends.
Inputs may be any that keep to these rules, and one draw needn't show every extreme that they name: lists[b, 0] = (0, s) with s <= min(2, b); lists[b, 1] = (max(b - r, 0), b + 1) with 0 <= r <= 2; r = 2 for every block b that is a multiple of 3; s = 2 is reached in every draw.
All inputs are finite; a program needn't handle non-finite values.
Results may differ from the reference program's by a relative error of at most 0.012.
The reference program's roundings to bfloat16 on the way (of `weights` and `dscores`) count: a program that leaves them out, or rounds other values in their place, can miss the bound.
Values may be sent and summed in bfloat16 or wider, within the bound.
No kernel may reach another device: no remote copies, remote signals or barrier semaphores. Data moves between devices by JAX's collectives and lax.ppermute only.
A program may use at most 128 MiB of HBM per device.

```python
import math
import jax
import jax.numpy as jnp
import numpy as np
from jax import lax

HEADS = 48
HD = 128
HF = 6144
BLK = 128
REACH = 2
SINK = 2
TOK_DEV = 384
TOKENS = 24576


def draw_queries(key, part):
    key = jax.random.fold_in(key, 11)
    result = jax.random.truncated_normal(key, -6.0, 6.0, (TOKENS, HF), jnp.float32)
    return result.astype(jnp.bfloat16)


def draw_keys(key, part):
    key = jax.random.fold_in(key, 13)
    result = jax.random.truncated_normal(key, -6.0, 6.0, (TOKENS, HF), jnp.float32)
    return result.astype(jnp.bfloat16)


def draw_lists(key, part):
    key = jax.random.fold_in(key, 5)
    sink_key, back_key, pick_key = jax.random.split(key, 3)
    blocks = TOKENS // BLK
    order = jnp.arange(blocks, dtype=jnp.int32)
    pick = jax.random.randint(pick_key, (), SINK, blocks)
    sink_end = jax.random.randint(sink_key, (blocks,), 0, SINK + 1)
    sink_end = jnp.where(order == pick, SINK, jnp.minimum(sink_end, order))
    back = jax.random.randint(back_key, (blocks,), 0, REACH + 1)
    back = jnp.where(order == pick, REACH, back)
    back = jnp.where(order % (TOK_DEV // BLK) == 0, REACH, back)
    start = jnp.maximum(order - back, 0)
    zeros = jnp.zeros_like(order)
    first = jnp.stack([zeros, sink_end], axis=-1)
    second = jnp.stack([start, order + 1], axis=-1)
    return jnp.stack([first, second], axis=1).astype(jnp.int32)


def levels(stream_key, shape, shards, least, largest):
    loudness, own = 1.0, jax.random.fold_in(stream_key, 6)
    for axis_at, parts in shards:
        steps = jnp.exp(jax.random.uniform(jax.random.fold_in(own, axis_at), (parts,), jnp.float32, least / len(shards), largest / len(shards)))
        loudness = loudness * jnp.repeat(steps, shape[axis_at] // parts).reshape([-1 if axis == axis_at else 1 for axis in range(len(shape))])
    return loudness


def length_profile(number_of, total, bound, lean):
    loads = [(1 << 20) // math.isqrt(standing ** lean) + 1 for standing in range(2, number_of + 1)]
    rest, holding = total - bound - (number_of - 1), [1] * (number_of - 1)
    while rest > 0:
        movable = [i for i in range(number_of - 1) if holding[i] < bound]
        mass, budget = sum([loads[i] for i in movable]), rest
        for i in movable:
            addition = min(bound - holding[i], max(1, budget * loads[i] // mass), rest)
            holding[i] = holding[i] + addition
            rest = rest - addition
    return np.array([bound] + holding)


def uneven_parts(own_key, count, total, bound, skew):
    if count == 2:
        one = jax.random.randint(own_key, (), max(1, total - bound), min(bound, total - 1) + 1)
        return jnp.stack([one, total - one])
    lengths = jnp.asarray(length_profile(count, total, bound, skew), jnp.int32)
    twos = (count - 1) // 2
    source_of, taker = lengths[1:1 + 2 * twos:2], lengths[2:2 + 2 * twos:2]
    margin = jnp.minimum(source_of - 1, bound - taker)
    shifted = jax.random.randint(jax.random.fold_in(own_key, 1), (twos,), 0, 1 << 20) % (margin + 1)
    lengths = lengths.at[1:1 + 2 * twos:2].set(source_of - shifted).at[2:2 + 2 * twos:2].set(taker + shifted)
    return lengths[jax.random.permutation(jax.random.fold_in(own_key, 2), count)]


def noise(own_key, dims, deviation, limit, pieces=(), held_as=jnp.bfloat16):
    loudness = levels(own_key, dims, pieces, -0.22, 0.18) if pieces else 1.0
    entries = jax.random.normal(own_key, dims, jnp.float32) * deviation * loudness
    return jnp.minimum(jnp.maximum(entries, -limit), limit).astype(held_as)


def setup_inputs(seed: int = 0) -> dict:
    key_of = jax.random.split(jax.random.key(seed), 7)
    queries = draw_queries(jax.random.fold_in(key_of[6], 71), 0)
    keys = draw_keys(jax.random.fold_in(key_of[6], 71), 0)
    values = noise(key_of[2], (TOKENS, HF), 1.0, 6.0, ((0, 256),))
    grad_out = noise(key_of[3], (TOKENS, HF), 1.0, 6.0, ((0, 256),))
    segment = jnp.searchsorted(jnp.cumsum(uneven_parts(key_of[4], 2 * TOKENS // BLK, TOKENS, 2 * BLK, 1)), jnp.arange(TOKENS), side="right").astype(jnp.int32)
    lists = draw_lists(jax.random.fold_in(key_of[6], 71), 0)
    return {"queries": queries, "keys": keys, "values": values, "grad_out": grad_out, "segment": segment, "lists": lists}


NEG = -1e+30

def rounded(x):
    return lax.optimization_barrier(x.astype(jnp.bfloat16)).astype(jnp.float32)

def allowed_of(lists, segment, q_index, q_block, k_index, k_block, k_valid):
    bounds = lists[q_block]
    first = (bounds[:, 0, 0][:, None] <= k_block[None, :]) & (k_block[None, :] < bounds[:, 0, 1][:, None])
    second = (bounds[:, 1, 0][:, None] <= k_block[None, :]) & (k_block[None, :] < bounds[:, 1, 1][:, None])
    order = (k_index[None, :] <= q_index[:, None]) | (segment[k_index][None, :] == segment[q_index][:, None])
    return (first | second) & order & k_valid[None, :]

def reference(queries, keys, values, grad_out, segment, lists):
    blocks = TOKENS // BLK
    scale = 1.0 / math.sqrt(HD)
    q_all = queries.reshape(TOKENS, HEADS, HD)
    k_all = keys.reshape(TOKENS, HEADS, HD)
    v_all = values.reshape(TOKENS, HEADS, HD)
    g_all = grad_out.reshape(TOKENS, HEADS, HD)
    span = jnp.arange(BLK, dtype=jnp.int32)
    window = REACH + 1

    def forward_block(q_blk):
        near = q_blk - REACH + jnp.arange(window, dtype=jnp.int32)
        far = jnp.arange(SINK, dtype=jnp.int32)
        k_blocks = jnp.concatenate([near, far])
        k_ok = jnp.concatenate([near >= 0, far < q_blk - REACH])
        k_index = (k_blocks[:, None] * BLK + span[None, :]).reshape(-1)
        k_index = jnp.clip(k_index, 0, TOKENS - 1).astype(jnp.int32)
        k_block_rows = jnp.repeat(k_blocks, BLK)
        k_valid = jnp.repeat(k_ok, BLK)
        q_index = (q_blk * BLK + span).astype(jnp.int32)
        q_block_rows = jnp.full((BLK,), q_blk, jnp.int32)
        allow = allowed_of(lists, segment, q_index, q_block_rows, k_index, k_block_rows, k_valid)
        qf = q_all[q_index].astype(jnp.float32)
        kf = k_all[k_index].astype(jnp.float32)
        vf = v_all[k_index].astype(jnp.float32)
        gf = g_all[q_index].astype(jnp.float32)
        scores = jnp.einsum('qhd,khd->hqk', qf, kf) * scale
        scores = jnp.where(allow[None], scores, NEG)
        top = lax.optimization_barrier(jnp.max(scores, axis=-1))
        lse = top + jnp.log(lax.optimization_barrier(jnp.sum(jnp.exp(scores - top[..., None]), axis=-1)))
        probs = jnp.exp(scores - lse[..., None])
        weights = rounded(probs)
        attended = jnp.einsum('hqk,khd->qhd', weights, vf).astype(jnp.bfloat16)
        delta = lax.optimization_barrier(jnp.sum(gf * attended.astype(jnp.float32), axis=-1)).T
        dprobs = jnp.einsum('qhd,khd->hqk', gf, vf)
        dscores = rounded(probs * (dprobs - delta[..., None]))
        grad_q = (scale * jnp.einsum('hqk,khd->qhd', dscores, kf)).astype(jnp.bfloat16)
        return (attended, grad_q, lse, delta)
    attended, grad_q, lse_all, delta_all = lax.map(forward_block, jnp.arange(blocks, dtype=jnp.int32))

    def window_block(k_blk):
        q_blocks = k_blk + jnp.arange(window, dtype=jnp.int32)
        q_ok = q_blocks < blocks
        q_safe = jnp.minimum(q_blocks, blocks - 1).astype(jnp.int32)
        q_index = (q_safe[:, None] * BLK + span[None, :]).reshape(-1).astype(jnp.int32)
        q_block_rows = jnp.repeat(q_safe, BLK)
        q_valid = jnp.repeat(q_ok, BLK)
        k_index = (k_blk * BLK + span).astype(jnp.int32)
        k_block_rows = jnp.full((BLK,), k_blk, jnp.int32)
        allow = allowed_of(lists, segment, q_index, q_block_rows, k_index, k_block_rows, jnp.ones((BLK,), bool))
        allow = allow & q_valid[:, None]
        qf = q_all[q_index].astype(jnp.float32)
        kf = k_all[k_index].astype(jnp.float32)
        vf = v_all[k_index].astype(jnp.float32)
        gf = g_all[q_index].astype(jnp.float32)
        lse = lse_all[q_safe].transpose(1, 0, 2).reshape(HEADS, window * BLK)
        delta = delta_all[q_safe].transpose(1, 0, 2).reshape(HEADS, window * BLK)
        scores = jnp.einsum('qhd,khd->hqk', qf, kf) * scale
        scores = jnp.where(allow[None], scores, NEG)
        probs = jnp.exp(scores - lse[..., None])
        weights = rounded(probs)
        grad_v = jnp.einsum('hqk,qhd->khd', weights, gf)
        dprobs = jnp.einsum('qhd,khd->hqk', gf, vf)
        dscores = rounded(probs * (dprobs - delta[..., None]))
        grad_k = scale * jnp.einsum('hqk,qhd->khd', dscores, qf)
        return (grad_k, grad_v)
    grad_k, grad_v = lax.map(window_block, jnp.arange(blocks, dtype=jnp.int32))
    grad_k = grad_k.reshape(TOKENS, HEADS, HD)
    grad_v = grad_v.reshape(TOKENS, HEADS, HD)
    sink_index = jnp.arange(SINK * BLK, dtype=jnp.int32)
    sink_blocks = sink_index // BLK
    kf_sink = k_all[sink_index].astype(jnp.float32)
    vf_sink = v_all[sink_index].astype(jnp.float32)

    def sink_step(carry, q_blk):
        acc_k, acc_v = carry
        q_index = (q_blk * BLK + span).astype(jnp.int32)
        q_block_rows = jnp.full((BLK,), q_blk, jnp.int32)
        k_valid = sink_blocks < q_blk - REACH
        allow = allowed_of(lists, segment, q_index, q_block_rows, sink_index, sink_blocks, k_valid)
        qf = q_all[q_index].astype(jnp.float32)
        gf = g_all[q_index].astype(jnp.float32)
        lse = lse_all[q_blk]
        delta = delta_all[q_blk]
        scores = jnp.einsum('qhd,khd->hqk', qf, kf_sink) * scale
        scores = jnp.where(allow[None], scores, NEG)
        probs = jnp.exp(scores - lse[..., None])
        weights = rounded(probs)
        dprobs = jnp.einsum('qhd,khd->hqk', gf, vf_sink)
        dscores = rounded(probs * (dprobs - delta[..., None]))
        acc_k = acc_k + scale * jnp.einsum('hqk,qhd->khd', dscores, qf)
        acc_v = acc_v + jnp.einsum('hqk,qhd->khd', weights, gf)
        return ((acc_k, acc_v), None)
    zero = jnp.zeros((SINK * BLK, HEADS, HD), jnp.float32)
    (sink_k, sink_v), _ = lax.scan(sink_step, (zero, zero), jnp.arange(blocks, dtype=jnp.int32))
    grad_k = grad_k.at[:SINK * BLK].add(sink_k)
    grad_v = grad_v.at[:SINK * BLK].add(sink_v)
    return (attended.reshape(TOKENS, HF), grad_q.reshape(TOKENS, HF), grad_k.reshape(TOKENS, HF).astype(jnp.bfloat16), grad_v.reshape(TOKENS, HF).astype(jnp.bfloat16))
```

```python
import functools
import math

import jax
import jax.numpy as jnp
from jax import lax
from jax.experimental import pallas as pl
from jax.experimental.pallas import tpu as pltpu
from jax.sharding import Mesh
from jax.sharding import PartitionSpec as P

HD = 128
BLK = 128
REACH = 2
SINK = 2
NEG = -1e30
LOG2E = 1.4426950408889634

TEAM = ("zi", "c", "x")
GROUPS = ("y", "zo")
NY, NZ = 4, 4
MEMBERS = 16
ROWS = 96
HEADS = 3
COLS = HEADS * HD
TOK = MEMBERS * ROWS
BLOCKS = TOK // BLK
EDGE = REACH * BLK
SPAN = EDGE + BLK
VMEM = 56 * 1024 * 1024


def params():
    return pltpu.CompilerParams(vmem_limit_bytes=VMEM)


def pack_kernel(a_ref, b_ref, out_ref):
    for i in range(out_ref.shape[0]):
        out_ref[i, 0] = a_ref[:, i * COLS : (i + 1) * COLS]
        out_ref[i, 1] = b_ref[:, i * COLS : (i + 1) * COLS]


def pack(a, b):
    per = 4
    spec = pl.BlockSpec((ROWS, per * COLS), lambda i: (0, i))
    return pl.pallas_call(
        pack_kernel,
        grid=(MEMBERS // per,),
        in_specs=[spec, spec],
        out_specs=pl.BlockSpec((per, 2, ROWS, COLS), lambda i: (i, 0, 0, 0)),
        out_shape=jax.ShapeDtypeStruct((MEMBERS, 2, ROWS, COLS), jnp.bfloat16),
        compiler_params=params(),
        cost_estimate=pl.CostEstimate(flops=0, bytes_accessed=4800000, transcendentals=0),
    )(a, b)


def unpack_kernel(in_ref, a_ref, b_ref):
    for i in range(in_ref.shape[0]):
        a_ref[:, i * COLS : (i + 1) * COLS] = in_ref[i, 0]
        b_ref[:, i * COLS : (i + 1) * COLS] = in_ref[i, 1]


def unpack(both):
    per = 4
    spec = pl.BlockSpec((ROWS, per * COLS), lambda i: (0, i))
    shape = jax.ShapeDtypeStruct((ROWS, MEMBERS * COLS), jnp.bfloat16)
    return pl.pallas_call(
        unpack_kernel,
        grid=(MEMBERS // per,),
        in_specs=[pl.BlockSpec((per, 2, ROWS, COLS), lambda i: (i, 0, 0, 0))],
        out_specs=[spec, spec],
        out_shape=[shape, shape],
        compiler_params=params(),
        cost_estimate=pl.CostEstimate(flops=0, bytes_accessed=4800000, transcendentals=0),
    )(both)


def exchange(both):
    return lax.all_to_all(both, TEAM, split_axis=0, concat_axis=0, tiled=True)


def dot(a, b, dims):
    return lax.dot_general(a, b, (dims, ((), ())), preferred_element_type=jnp.float32)


def attention_kernel(
    lists_ref,
    first_ref,
    kv_ref,
    qg_ref,
    prior_ref,
    sink_k_ref,
    sink_v_ref,
    seg_ref,
    out_ref,
    grads_ref,
    prior_out_ref,
    sink_out_ref,
    kx,
    vx,
    qx,
    gx,
    ax,
    dqx,
    dk,
    dv,
):
    step = pl.program_id(0)
    scale = 1.0 / math.sqrt(HD)

    @pl.when(step == 0)
    def _():
        skip = 3 * ROWS - EDGE
        kx[: ROWS - skip] = prior_ref[0, 0, skip:]
        vx[: ROWS - skip] = prior_ref[0, 1, skip:]
        for i in (1, 2):
            kx[i * ROWS - skip : (i + 1) * ROWS - skip] = prior_ref[i, 0]
            vx[i * ROWS - skip : (i + 1) * ROWS - skip] = prior_ref[i, 1]
        for i in range(MEMBERS):
            kx[EDGE + i * ROWS : EDGE + (i + 1) * ROWS] = kv_ref[i, 0]
            vx[EDGE + i * ROWS : EDGE + (i + 1) * ROWS] = kv_ref[i, 1]
            qx[i * ROWS : (i + 1) * ROWS] = qg_ref[i, 0]
            gx[i * ROWS : (i + 1) * ROWS] = qg_ref[i, 1]
        dk[...] = jnp.zeros_like(dk)
        dv[...] = jnp.zeros_like(dv)
        sink_out_ref[...] = jnp.zeros_like(sink_out_ref)

    here = first_ref[0] + step

    def listed(block):
        one = (lists_ref[step, 0] <= block) & (block < lists_ref[step, 1])
        two = (lists_ref[step, 2] <= block) & (block < lists_ref[step, 3])
        return one | two

    def bias(ok):
        return jnp.where(ok, 0.0, NEG).astype(jnp.float32)

    sink_bias = [bias(listed(i) & (i < here - REACH)) for i in range(SINK)]
    near_bias = [bias(listed(here - REACH + i) & (here - REACH + i >= 0)) for i in range(REACH)]
    seg_row = jnp.broadcast_to(seg_ref[pl.ds(step, 1), :], (BLK, BLK))
    row = lax.broadcasted_iota(jnp.int32, (BLK, BLK), 0)
    col = lax.broadcasted_iota(jnp.int32, (BLK, BLK), 1)
    order = (col <= row) | (seg_row == seg_row.T)
    own = jnp.where(order & listed(here), 0.0, NEG)

    rows = pl.ds(pl.multiple_of(step * BLK, BLK), BLK)
    span = pl.ds(pl.multiple_of(step * BLK, BLK), SPAN)
    parts = SINK + REACH + 1
    for h in range(HEADS):
        at = slice(h * HD, (h + 1) * HD)
        q, g = qx[rows, at], gx[rows, at]
        k_near, v_near = kx[span, at], vx[span, at]
        k_far = jnp.concatenate([sink_k_ref[0, :, at], sink_k_ref[1, :, at], sink_k_ref[2, :, at]])[:EDGE]
        v_far = jnp.concatenate([sink_v_ref[0, :, at], sink_v_ref[1, :, at], sink_v_ref[2, :, at]])[:EDGE]
        s_far = dot(q, k_far, ((1,), (1,))) * (scale * LOG2E)
        s_near = dot(q, k_near, ((1,), (1,))) * (scale * LOG2E)
        s = [s_far[:, i * BLK : (i + 1) * BLK] + sink_bias[i] for i in range(SINK)]
        s += [s_near[:, i * BLK : (i + 1) * BLK] + near_bias[i] for i in range(REACH)]
        s += [s_near[:, EDGE:] + own]
        top = jnp.max(functools.reduce(jnp.maximum, s), axis=-1, keepdims=True)
        e = [jnp.exp2(x - top) for x in s]
        inv = 1.0 / jnp.sum(functools.reduce(jnp.add, e), axis=-1, keepdims=True)
        p = [x * inv for x in e]
        w = [x.astype(jnp.bfloat16) for x in p]
        w_far = jnp.concatenate(w[:SINK], axis=1)
        w_near = jnp.concatenate(w[SINK:], axis=1)
        att = dot(w_far, v_far, ((1,), (0,))) + dot(w_near, v_near, ((1,), (0,)))
        att = att.astype(jnp.bfloat16)
        delta = jnp.sum(g.astype(jnp.float32) * att.astype(jnp.float32), axis=-1, keepdims=True)
        dp_far = dot(g, v_far, ((1,), (1,)))
        dp_near = dot(g, v_near, ((1,), (1,)))
        dp = [dp_far[:, i * BLK : (i + 1) * BLK] for i in range(SINK)]
        dp += [dp_near[:, i * BLK : (i + 1) * BLK] for i in range(REACH + 1)]
        ds = [(p[i] * (dp[i] - delta)).astype(jnp.bfloat16) for i in range(parts)]
        ds_far = jnp.concatenate(ds[:SINK], axis=1)
        ds_near = jnp.concatenate(ds[SINK:], axis=1)
        dq = dot(ds_far, k_far, ((1,), (0,))) + dot(ds_near, k_near, ((1,), (0,)))
        ax[rows, at] = att
        dqx[rows, at] = (scale * dq).astype(jnp.bfloat16)
        dk[span, at] += dot(ds_near, q, ((0,), (0,)))
        dv[span, at] += dot(w_near, g, ((0,), (0,)))
        sink_out_ref[0, :, at] += dot(ds_far, q, ((0,), (0,)))
        sink_out_ref[1, :, at] += dot(w_far, g, ((0,), (0,)))

    @pl.when(step == BLOCKS - 1)
    def _():
        sink_out_ref[0] = sink_out_ref[0] * scale
        prior_out_ref[0] = (dk[:EDGE] * scale).astype(jnp.bfloat16)
        prior_out_ref[1] = dv[:EDGE].astype(jnp.bfloat16)
        grads_ref[0] = dk[EDGE:] * scale
        grads_ref[1] = dv[EDGE:]
        for i in range(MEMBERS):
            out_ref[i, 0] = ax[i * ROWS : (i + 1) * ROWS]
            out_ref[i, 1] = dqx[i * ROWS : (i + 1) * ROWS]


def attention(lists, first, kv, qg, prior, sink_k, sink_v, seg):
    def whole(shape):
        return pl.BlockSpec(shape, lambda i, *_: (0,) * len(shape))

    shapes = [
        jax.ShapeDtypeStruct((MEMBERS, 2, ROWS, COLS), jnp.bfloat16),
        jax.ShapeDtypeStruct((2, TOK, COLS), jnp.float32),
        jax.ShapeDtypeStruct((2, EDGE, COLS), jnp.bfloat16),
        jax.ShapeDtypeStruct((2, EDGE, COLS), jnp.float32),
    ]
    tokens = pltpu.VMEM((TOK, COLS), jnp.bfloat16)
    wide = pltpu.VMEM((EDGE + TOK, COLS), jnp.bfloat16)
    total = pltpu.VMEM((EDGE + TOK, COLS), jnp.float32)
    return pl.pallas_call(
        attention_kernel,
        grid_spec=pltpu.PrefetchScalarGridSpec(
            num_scalar_prefetch=2,
            grid=(BLOCKS,),
            in_specs=[whole(x.shape) for x in (kv, qg, prior, sink_k, sink_v, seg)],
            out_specs=[whole(x.shape) for x in shapes],
            scratch_shapes=[wide, wide, tokens, tokens, tokens, tokens, total, total],
        ),
        out_shape=shapes,
        compiler_params=params(),
        cost_estimate=pl.CostEstimate(flops=8000000000, bytes_accessed=16000000, transcendentals=3000000),
    )(lists, first, kv, qg, prior, sink_k, sink_v, seg)


def finish_kernel(owner_ref, grads_ref, back_ref, sink_k_ref, sink_v_ref, out_ref):
    keep = owner_ref[0].astype(jnp.float32)
    for n, sink_ref in ((0, sink_k_ref), (1, sink_v_ref)):
        for i in range(MEMBERS):
            start = i * ROWS
            piece = grads_ref[n, start : start + ROWS]
            if start < EDGE:
                have = min(ROWS, EDGE - start)
                add = sink_ref[start : start + have] * keep
                piece = jnp.concatenate([piece[:have] + add, piece[have:]]) if have < ROWS else piece + add
            tail = TOK - EDGE
            if start + ROWS > tail:
                lead = max(0, tail - start)
                add = back_ref[n, start + lead - tail : start + ROWS - tail].astype(jnp.float32)
                piece = jnp.concatenate([piece[:lead], piece[lead:] + add]) if lead else piece + add
            out_ref[i, n] = piece.astype(jnp.bfloat16)


def finish(owner, grads, back, sink_k, sink_v):
    vmem = pl.BlockSpec(memory_space=pltpu.VMEM)
    return pl.pallas_call(
        finish_kernel,
        in_specs=[pl.BlockSpec(memory_space=pltpu.SMEM), vmem, vmem, vmem, vmem],
        out_specs=vmem,
        out_shape=jax.ShapeDtypeStruct((MEMBERS, 2, ROWS, COLS), jnp.bfloat16),
        compiler_params=params(),
        cost_estimate=pl.CostEstimate(flops=1000000, bytes_accessed=8000000, transcendentals=0),
    )(owner, grads, back, sink_k, sink_v)


def send(value, pairs):
    return lax.ppermute(value, GROUPS, pairs)


def fan_out(value, pairs_of, mine):
    got = [send(value, pairs_of(d)) for d in (1, 2, 3)]
    return jnp.where(mine, value, got[0] + got[1] + got[2])


def fan_in(total, pairs_of):
    sent = total.astype(jnp.bfloat16)
    got = [send(sent, pairs_of(d)).astype(jnp.float32) for d in (1, 2, 3)]
    return total + got[0] + got[1] + got[2]


def per_device(queries, keys, values, grad_out, segment, lists):
    y, zo = lax.axis_index("y"), lax.axis_index("zo")
    group = y * NZ + zo
    small = jnp.concatenate([segment, lists.reshape(-1), jnp.zeros((116,), jnp.int32)])
    small = lax.all_gather(small, ("zi", "c"), axis=0, tiled=False).reshape(4, 512)
    seg = small[:, :384].reshape(BLOCKS, BLK).astype(jnp.float32)
    bounds = small[:, 384:396].reshape(BLOCKS, 4)

    kv = exchange(pack(keys, values))
    qg = exchange(pack(queries, grad_out))

    prior = send(kv[MEMBERS - 3 :], [(i, i + 1) for i in range(NY * NZ - 1)])
    root_k, root_v = kv[:3, 0], kv[:3, 1]
    sink_k = fan_out(root_k, lambda d: [(0, d)], zo == 0)
    sink_k = fan_out(sink_k, lambda d: [(i, d * NZ + i) for i in range(NZ)], y == 0)
    sink_v = fan_out(root_v, lambda d: [(0, d * NZ)], y == 0)
    sink_v = fan_out(sink_v, lambda d: [(j * NZ, j * NZ + d) for j in range(NY)], zo == 0)

    first = (group * BLOCKS).reshape(1)
    out, grads, prior_out, sink_out = attention(bounds, first, kv, qg, prior, sink_k, sink_v, seg)

    back = send(prior_out, [(i + 1, i) for i in range(NY * NZ - 1)])
    total_k = fan_in(sink_out[0], lambda d: [(j * NZ + d, j * NZ) for j in range(NY)])
    total_k = fan_in(total_k, lambda d: [(d * NZ, 0)])
    total_v = fan_in(sink_out[1], lambda d: [(d * NZ + i, i) for i in range(NZ)])
    total_v = fan_in(total_v, lambda d: [(d, 0)])

    attended, grad_q = unpack(exchange(out))
    owner = (group == 0).astype(jnp.int32).reshape(1)
    grad_k, grad_v = unpack(exchange(finish(owner, grads, back, total_k, total_v)))
    return attended, grad_q, grad_k, grad_v


def solution(mesh):
    fine = Mesh(mesh.devices.reshape(NY, NZ, 2, 2, 4), ("y", "zo", "zi", "c", "x"))
    rows = P(("y", "zo", "zi", "c", "x"), None)
    ctx = ("y", "zo", "zi", "c")
    return jax.shard_map(
        per_device,
        mesh=fine,
        in_specs=(rows, rows, rows, rows, P(ctx), P(ctx, None, None)),
        out_specs=(rows, rows, rows, rows),
        check_vma=False,
    )
```

```python
import functools
import math

import jax
import jax.numpy as jnp
from jax import lax
from jax.experimental import pallas as pl
from jax.experimental.pallas import tpu as pltpu
from jax.sharding import Mesh
from jax.sharding import PartitionSpec as P

HD = 128
BLK = 128
REACH = 2
SINK = 2
NEG = -1e30
LOG2E = 1.4426950408889634

TEAM = ("zi", "c", "x")
GROUPS = ("y", "zo")
NY, NZ = 4, 4
MEMBERS = 16
ROWS = 96
HEADS = 3
COLS = HEADS * HD
TOK = MEMBERS * ROWS
BLOCKS = TOK // BLK
EDGE = REACH * BLK
SPAN = EDGE + BLK
EDGE_ROWS = 3 * ROWS
EDGES = (0, 1, 2, 13, 14, 15)
WORK = 3
CHUNKS = WORK * BLK // ROWS
HALF = 16
VMEM = 56 * 1024 * 1024


def params():
    return pltpu.CompilerParams(vmem_limit_bytes=VMEM)


def pack_kernel(a_ref, b_ref, out_ref):
    for i in range(out_ref.shape[0]):
        out_ref[i, 0] = a_ref[:, i * COLS : (i + 1) * COLS]
        out_ref[i, 1] = b_ref[:, i * COLS : (i + 1) * COLS]


def pack(a, b):
    per = 2
    spec = pl.BlockSpec((ROWS, per * COLS), lambda i: (0, i))
    return pl.pallas_call(
        pack_kernel,
        grid=(MEMBERS // per,),
        in_specs=[spec, spec],
        out_specs=pl.BlockSpec((per, 2, ROWS, COLS), lambda i: (i, 0, 0, 0)),
        out_shape=jax.ShapeDtypeStruct((MEMBERS, 2, ROWS, COLS), jnp.bfloat16),
        compiler_params=params(),
        cost_estimate=pl.CostEstimate(flops=0, bytes_accessed=4800000, transcendentals=0),
    )(a, b)


def unpack_kernel(in_ref, a_ref, b_ref):
    for i in range(in_ref.shape[0]):
        a_ref[:, i * COLS : (i + 1) * COLS] = in_ref[i, 0]
        b_ref[:, i * COLS : (i + 1) * COLS] = in_ref[i, 1]


def unpack(both):
    per = 2
    spec = pl.BlockSpec((ROWS, per * COLS), lambda i: (0, i))
    shape = jax.ShapeDtypeStruct((ROWS, MEMBERS * COLS), jnp.bfloat16)
    return pl.pallas_call(
        unpack_kernel,
        grid=(MEMBERS // per,),
        in_specs=[pl.BlockSpec((per, 2, ROWS, COLS), lambda i: (i, 0, 0, 0))],
        out_specs=[spec, spec],
        out_shape=[shape, shape],
        compiler_params=params(),
        cost_estimate=pl.CostEstimate(flops=0, bytes_accessed=4800000, transcendentals=0),
    )(both)


def exchange(both):
    return lax.all_to_all(both, TEAM, split_axis=0, concat_axis=0, tiled=True)


def dot(a, b, dims):
    return lax.dot_general(a, b, (dims, ((), ())), preferred_element_type=jnp.float32)


def attention_kernel(
    lists_ref,
    first_ref,
    kv_ref,
    qg_ref,
    prior_ref,
    sink_k_ref,
    sink_v_ref,
    seg_ref,
    out_ref,
    grads_ref,
    edges_ref,
    prior_out_ref,
    sink_out_ref,
    kx,
    vx,
    kt,
    vt,
    kt_far,
    vt_far,
    totals,
):
    step = pl.program_id(0)
    scale = 1.0 / math.sqrt(HD)
    skip = EDGE_ROWS - EDGE

    @pl.when(step == 0)
    def _():
        for n, x in ((0, kx), (1, vx)):
            x[: ROWS - skip] = prior_ref[0, n, skip:]
            for i in (1, 2):
                x[i * ROWS - skip : (i + 1) * ROWS - skip] = prior_ref[i, n]
        for h in range(HEADS):
            at = slice(h * HD, (h + 1) * HD)
            kt_far[at] = sink_k_ref[:EDGE, at].T
            vt_far[at] = sink_v_ref[:EDGE, at].T
            kt[at, :EDGE] = kx[:EDGE, at].T
            vt[at, :EDGE] = vx[:EDGE, at].T
        totals[:, :EDGE] = jnp.zeros((2, EDGE, COLS), jnp.float32)
        sink_out_ref[...] = jnp.zeros_like(sink_out_ref)
        prior_out_ref[:, :skip] = jnp.zeros((2, skip, COLS), jnp.bfloat16)

    for n, x in ((0, kx), (1, vx)):
        for i in range(CHUNKS):
            x[EDGE + i * ROWS : EDGE + (i + 1) * ROWS] = kv_ref[i, n]

    key = lax.broadcasted_iota(jnp.int32, (BLK, BLK), 0)
    query = lax.broadcasted_iota(jnp.int32, (BLK, BLK), 1)

    def bias(ok):
        return jnp.where(ok, 0.0, NEG).astype(jnp.float32)

    masks = []
    for u in range(WORK):
        at_block = step * WORK + u
        here = first_ref[0] + at_block

        def listed(block, at_block=at_block):
            one = (lists_ref[at_block, 0] <= block) & (block < lists_ref[at_block, 1])
            two = (lists_ref[at_block, 2] <= block) & (block < lists_ref[at_block, 3])
            return one | two

        far = [bias(listed(i) & (i < here - REACH)) for i in range(SINK)]
        near = [here - REACH + i for i in range(REACH)]
        near = [bias(listed(x) & (x >= 0)) for x in near]
        seg_row = jnp.broadcast_to(seg_ref[pl.ds(at_block, 1), :], (BLK, BLK))
        order = (key <= query) | (seg_row == seg_row.T)
        masks.append(far + near + [jnp.where(order & listed(here), 0.0, NEG)])

    def blocks(x):
        return [x[i * BLK : (i + 1) * BLK] for i in range(x.shape[0] // BLK)]

    for h in range(HEADS):
        at = slice(h * HD, (h + 1) * HD)
        q_all = qg_ref[:, 0, :, at].reshape(WORK * BLK, HD)
        g_all = qg_ref[:, 1, :, at].reshape(WORK * BLK, HD)
        kt[at, EDGE:] = kx[EDGE:, at].T
        vt[at, EDGE:] = vx[EDGE:, at].T
        g_turned = g_all.astype(jnp.float32).T
        qs, gs = blocks(q_all), blocks(g_all)
        k_far, v_far = sink_k_ref[:EDGE, at], sink_v_ref[:EDGE, at]
        s_far = dot(k_far, q_all, ((1,), (1,)))
        dp_far = dot(v_far, g_all, ((1,), (1,)))
        ps, ws = [], []
        for u in range(WORK):
            lanes = slice(u * BLK, (u + 1) * BLK)
            span = slice(u * BLK, u * BLK + SPAN)
            s = blocks(s_far[:, lanes]) + blocks(dot(kx[span, at], qs[u], ((1,), (1,))))
            s = [x * (scale * LOG2E) + y for x, y in zip(s, masks[u])]
            top = jnp.max(functools.reduce(jnp.maximum, s), axis=0, keepdims=True)
            e = [jnp.exp2(x - top) for x in s]
            inv = 1.0 / jnp.sum(functools.reduce(jnp.add, e), axis=0, keepdims=True)
            p = [x * inv for x in e]
            ps.append(p)
            ws.append([x.astype(jnp.bfloat16) for x in p])
        w_far = jnp.concatenate([jnp.concatenate(w[:SINK], axis=0) for w in ws], axis=1)
        att_far = dot(vt_far[at, :], w_far, ((1,), (0,)))
        dss, atts = [], []
        for u in range(WORK):
            lanes = slice(u * BLK, (u + 1) * BLK)
            span = slice(u * BLK, u * BLK + SPAN)
            w_near = jnp.concatenate(ws[u][SINK:], axis=0)
            att = att_far[:, lanes] + dot(vt[at, span], w_near, ((1,), (0,)))
            att = att.astype(jnp.bfloat16).astype(jnp.float32)
            atts.append(att)
            delta = jnp.sum(g_turned[:, lanes] * att, axis=0, keepdims=True)
            dp = blocks(dp_far[:, lanes]) + blocks(dot(vx[span, at], gs[u], ((1,), (1,))))
            dss.append([(x * (y - delta)).astype(jnp.bfloat16) for x, y in zip(ps[u], dp)])
        ds_far = jnp.concatenate([jnp.concatenate(ds[:SINK], axis=0) for ds in dss], axis=1)
        dq_far = dot(kt_far[at, :], ds_far, ((1,), (0,)))
        dqs = []
        for u in range(WORK):
            lanes = slice(u * BLK, (u + 1) * BLK)
            span = slice(u * BLK, u * BLK + SPAN)
            ds_near = jnp.concatenate(dss[u][SINK:], axis=0)
            dqs.append(dq_far[:, lanes] + dot(kt[at, span], ds_near, ((1,), (0,))))
        att = jnp.concatenate(atts, axis=1).T.astype(jnp.bfloat16)
        dq = (scale * jnp.concatenate(dqs, axis=1)).T.astype(jnp.bfloat16)
        out_ref[:, 0, :, at] = att.reshape(CHUNKS, ROWS, HD)
        out_ref[:, 1, :, at] = dq.reshape(CHUNKS, ROWS, HD)
        sink_out_ref[0, :EDGE, at] += dot(ds_far, q_all, ((1,), (0,))) * scale
        sink_out_ref[1, :EDGE, at] += dot(w_far, g_all, ((1,), (0,)))
        for j in range(WORK + REACH):
            used = [u for u in range(WORK) if 0 <= j - u <= REACH]
            lanes = slice(used[0] * BLK, (used[-1] + 1) * BLK)
            ds = jnp.concatenate([dss[u][SINK + j - u] for u in used], axis=1)
            w = jnp.concatenate([ws[u][SINK + j - u] for u in used], axis=1)
            dk = dot(ds, q_all[lanes], ((1,), (0,))) * scale
            dv = dot(w, g_all[lanes], ((1,), (0,)))
            row = slice(j * BLK, (j + 1) * BLK)
            if j < REACH:
                totals[0, row, at] += dk
                totals[1, row, at] += dv
            else:
                totals[0, row, at] = dk
                totals[1, row, at] = dv

    lead = step * CHUNKS
    for n in range(2):

        @pl.when(step == 0)
        def _(n=n):
            prior_out_ref[n, skip:] = totals[n, :EDGE].astype(jnp.bfloat16)

        @pl.when(step > 0)
        def _(n=n):
            grads_ref[lead - 3, n, 2 * HALF :] = totals[n, : 4 * HALF].astype(jnp.bfloat16)
            for i in (1, 2):
                start = 4 * HALF + (i - 1) * ROWS
                grads_ref[lead - 3 + i, n] = totals[n, start : start + ROWS].astype(jnp.bfloat16)

        body = totals[n, EDGE : EDGE + BLK]
        grads_ref[lead, n] = body[:ROWS].astype(jnp.bfloat16)
        grads_ref[lead + 1, n, : 2 * HALF] = body[ROWS:].astype(jnp.bfloat16)

        @pl.when(step == 0)
        def _(n=n):
            edges_ref[0, n] = totals[n, EDGE : EDGE + ROWS]
            edges_ref[1, n, : 2 * HALF] = totals[n, EDGE + ROWS : EDGE + BLK]

        @pl.when(step == 1)
        def _(n=n):
            edges_ref[1, n, 2 * HALF :] = totals[n, : 4 * HALF]
            edges_ref[2, n] = totals[n, 4 * HALF : 4 * HALF + ROWS]

        @pl.when(step == BLOCKS // WORK - 1)
        def _(n=n):
            edges_ref[3, n, : 2 * HALF] = totals[n, EDGE + ROWS : EDGE + BLK]
            edges_ref[3, n, 2 * HALF :] = totals[n, EDGE + BLK : EDGE + BLK + 4 * HALF]
            for i in (1, 2):
                start = EDGE + BLK + 4 * HALF + (i - 1) * ROWS
                edges_ref[3 + i, n] = totals[n, start : start + ROWS]
            for i in range(3):
                grads_ref[MEMBERS - 3 + i, n] = edges_ref[3 + i, n].astype(jnp.bfloat16)

    kx[:EDGE] = kx[WORK * BLK :]
    vx[:EDGE] = vx[WORK * BLK :]
    kt[:, :EDGE] = kt[:, WORK * BLK :]
    vt[:, :EDGE] = vt[:, WORK * BLK :]
    totals[:, :EDGE] = totals[:, WORK * BLK :]


def attention(lists, first, kv, qg, prior, sink_k, sink_v, seg):
    def whole(shape):
        return pl.BlockSpec(shape, lambda i, *_: (0,) * len(shape))

    shapes = [
        jax.ShapeDtypeStruct((MEMBERS, 2, ROWS, COLS), jnp.bfloat16),
        jax.ShapeDtypeStruct((MEMBERS, 2, ROWS, COLS), jnp.bfloat16),
        jax.ShapeDtypeStruct((len(EDGES), 2, ROWS, COLS), jnp.float32),
        jax.ShapeDtypeStruct((2, EDGE_ROWS, COLS), jnp.bfloat16),
        jax.ShapeDtypeStruct((2, EDGE_ROWS, COLS), jnp.float32),
    ]
    moving = pl.BlockSpec((CHUNKS, 2, ROWS, COLS), lambda i, *_: (i, 0, 0, 0))
    length = EDGE + WORK * BLK
    wide = pltpu.VMEM((length, COLS), jnp.bfloat16)
    turned = pltpu.VMEM((COLS, length), jnp.bfloat16)
    turned_far = pltpu.VMEM((COLS, EDGE), jnp.bfloat16)
    return pl.pallas_call(
        attention_kernel,
        grid_spec=pltpu.PrefetchScalarGridSpec(
            num_scalar_prefetch=2,
            grid=(BLOCKS // WORK,),
            in_specs=[moving, moving] + [whole(x.shape) for x in (prior, sink_k, sink_v, seg)],
            out_specs=[moving] + [whole(x.shape) for x in shapes[1:]],
            scratch_shapes=[
                wide,
                wide,
                turned,
                turned,
                turned_far,
                turned_far,
                pltpu.VMEM((2, length, COLS), jnp.float32),
            ],
        ),
        out_shape=shapes,
        compiler_params=params(),
        cost_estimate=pl.CostEstimate(flops=8000000000, bytes_accessed=16000000, transcendentals=3000000),
    )(lists, first, kv, qg, prior, sink_k, sink_v, seg)


def finish_kernel(owner_ref, grads_ref, edges_ref, back_ref, sink_k_ref, sink_v_ref, out_ref):
    del grads_ref
    keep = owner_ref[0].astype(jnp.float32)
    step = pl.program_id(0)

    @pl.when(step < 3)
    def _():
        out_ref[0, 0] = (edges_ref[0, 0] + sink_k_ref[0] * keep).astype(jnp.bfloat16)
        out_ref[0, 1] = (edges_ref[0, 1] + sink_v_ref[0] * keep).astype(jnp.bfloat16)

    @pl.when(step >= 3)
    def _():
        for n in range(2):
            out_ref[0, n] = (edges_ref[0, n] + back_ref[n, 0].astype(jnp.float32)).astype(jnp.bfloat16)


def finish(owner, grads, edges, back, sink_k, sink_v):
    back = back.reshape(2, 3, ROWS, COLS)
    sink_k = sink_k.reshape(3, ROWS, COLS)
    sink_v = sink_v.reshape(3, ROWS, COLS)
    sink_spec = pl.BlockSpec((1, ROWS, COLS), lambda i: (jnp.minimum(i, 2), 0, 0))
    return pl.pallas_call(
        finish_kernel,
        grid=(len(EDGES),),
        in_specs=[
            pl.BlockSpec(memory_space=pltpu.SMEM),
            pl.BlockSpec(memory_space=pl.ANY),
            pl.BlockSpec((1, 2, ROWS, COLS), lambda i: (i, 0, 0, 0)),
            pl.BlockSpec((2, 1, ROWS, COLS), lambda i: (0, jnp.maximum(i - 3, 0), 0, 0)),
            sink_spec,
            sink_spec,
        ],
        out_specs=pl.BlockSpec(
            (1, 2, ROWS, COLS), lambda i: (jnp.where(i < 3, i, i + MEMBERS - 6), 0, 0, 0)
        ),
        out_shape=jax.ShapeDtypeStruct((MEMBERS, 2, ROWS, COLS), jnp.bfloat16),
        input_output_aliases={1: 0},
        compiler_params=params(),
        cost_estimate=pl.CostEstimate(flops=1000000, bytes_accessed=4000000, transcendentals=0),
    )(owner, grads, edges, back, sink_k, sink_v)


def send(value, pairs):
    return lax.ppermute(value, GROUPS, pairs)


def later(value, earlier):
    return value + (earlier[(0,) * earlier.ndim] * 0).astype(value.dtype)


def fan_out(value, pairs_of, mine):
    got = [send(value, pairs_of(d)) for d in (1, 2, 3)]
    return jnp.where(mine, value, got[0] + got[1] + got[2])


def fan_in(total, pairs_of):
    sent = total.astype(jnp.bfloat16)
    got = [send(sent, pairs_of(d)).astype(jnp.float32) for d in (1, 2, 3)]
    return total + got[0] + got[1] + got[2]


def swapped(value, axis):
    other = lax.ppermute(value, axis, [(0, 1), (1, 0)])
    first = lax.axis_index(axis) == 0
    return jnp.concatenate([jnp.where(first, value, other), jnp.where(first, other, value)])


def per_device(queries, keys, values, grad_out, segment, lists):
    y, zo = lax.axis_index("y"), lax.axis_index("zo")
    group = y * NZ + zo
    small = jnp.concatenate([segment, lists.reshape(-1), jnp.zeros((116,), jnp.int32)])
    small = swapped(swapped(small.reshape(1, 512), "c"), "zi")
    seg = small[:, :384].reshape(BLOCKS, BLK).astype(jnp.float32)
    bounds = small[:, 384:396].reshape(BLOCKS, 4)

    kv = exchange(pack(keys, values))
    qg = exchange(pack(queries, grad_out))

    prior = send(kv[MEMBERS - 3 :], [(i, i + 1) for i in range(NY * NZ - 1)])
    root_k = kv[:3, 0].reshape(EDGE_ROWS, COLS)
    root_v = kv[:3, 1].reshape(EDGE_ROWS, COLS)
    sink_k = later(fan_out(root_k, lambda d: [(0, d)], zo == 0), prior)
    sink_v = later(fan_out(root_v, lambda d: [(0, d * NZ)], y == 0), prior)
    sink_k = fan_out(sink_k, lambda d: [(i, d * NZ + i) for i in range(NZ)], y == 0)
    sink_v = fan_out(sink_v, lambda d: [(j * NZ, j * NZ + d) for j in range(NY)], zo == 0)

    first = (group * BLOCKS).reshape(1)
    out, grads, edges, prior_out, sink_out = attention(
        bounds, first, kv, qg, prior, sink_k, sink_v, seg
    )

    back = send(prior_out, [(i + 1, i) for i in range(NY * NZ - 1)])
    total_k = later(fan_in(sink_out[0], lambda d: [(j * NZ + d, j * NZ) for j in range(NY)]), back)
    total_v = later(fan_in(sink_out[1], lambda d: [(d * NZ + i, i) for i in range(NZ)]), back)
    total_k = fan_in(total_k, lambda d: [(d * NZ, 0)])
    total_v = fan_in(total_v, lambda d: [(d, 0)])

    attended, grad_q = unpack(exchange(out))
    owner = (group == 0).astype(jnp.int32).reshape(1)
    grad_k, grad_v = unpack(exchange(finish(owner, grads, edges, back, total_k, total_v)))
    return attended, grad_q, grad_k, grad_v


def solution(mesh):
    fine = Mesh(mesh.devices.reshape(NY, NZ, 2, 2, 4), ("y", "zo", "zi", "c", "x"))
    rows = P(("y", "zo", "zi", "c", "x"), None)
    ctx = ("y", "zo", "zi", "c")
    return jax.shard_map(
        per_device,
        mesh=fine,
        in_specs=(rows, rows, rows, rows, P(ctx), P(ctx, None, None)),
        out_specs=(rows, rows, rows, rows),
        check_vma=False,
    )
```

```python
import functools
import math

import jax
import jax.numpy as jnp
from jax import lax
from jax.experimental import pallas as pl
from jax.experimental.pallas import tpu as pltpu
from jax.sharding import Mesh
from jax.sharding import PartitionSpec as P

HD = 128
BLK = 128
REACH = 2
SINK = 2
NEG = -1e30
LOG2E = 1.4426950408889634

TEAM = ("yi", "c", "x")
GROUPS = ("yo", "z")
NYO, NZ = 2, 8
MEMBERS = 16
ROWS = 96
HEADS = 3
COLS = HEADS * HD
TOK = MEMBERS * ROWS
BLOCKS = TOK // BLK
RUNS = 2
EDGE = REACH * BLK
SPAN = EDGE + BLK
WORK = 3
STEPS = BLOCKS // WORK
PER_RUN = STEPS // RUNS
CHUNKS = WORK * BLK // ROWS
RUN_CHUNKS = MEMBERS // RUNS
PART = EDGE - 2 * ROWS
REST = ROWS - PART
PER = 8
VMEM = 56 * 1024 * 1024


def params():
    return pltpu.CompilerParams(vmem_limit_bytes=VMEM)


def pack_kernel(a_ref, b_ref, out_ref):
    for i in range(out_ref.shape[0]):
        out_ref[i, 0] = a_ref[:, i * COLS : (i + 1) * COLS]
        out_ref[i, 1] = b_ref[:, i * COLS : (i + 1) * COLS]


def pack(a, b):
    per = PER
    spec = pl.BlockSpec((ROWS, per * COLS), lambda i: (0, i))
    return pl.pallas_call(
        pack_kernel,
        grid=(MEMBERS // per,),
        in_specs=[spec, spec],
        out_specs=pl.BlockSpec((per, 2, ROWS, COLS), lambda i: (i, 0, 0, 0)),
        out_shape=jax.ShapeDtypeStruct((MEMBERS, 2, ROWS, COLS), jnp.bfloat16),
        compiler_params=params(),
        cost_estimate=pl.CostEstimate(flops=0, bytes_accessed=4800000, transcendentals=0),
    )(a, b)


def unpack_kernel(in_ref, a_ref, b_ref):
    for i in range(in_ref.shape[0]):
        a_ref[:, i * COLS : (i + 1) * COLS] = in_ref[i, 0]
        b_ref[:, i * COLS : (i + 1) * COLS] = in_ref[i, 1]


def unpack(both):
    per = PER
    spec = pl.BlockSpec((ROWS, per * COLS), lambda i: (0, i))
    shape = jax.ShapeDtypeStruct((ROWS, MEMBERS * COLS), jnp.bfloat16)
    return pl.pallas_call(
        unpack_kernel,
        grid=(MEMBERS // per,),
        in_specs=[pl.BlockSpec((per, 2, ROWS, COLS), lambda i: (i, 0, 0, 0))],
        out_specs=[spec, spec],
        out_shape=[shape, shape],
        compiler_params=params(),
        cost_estimate=pl.CostEstimate(flops=0, bytes_accessed=4800000, transcendentals=0),
    )(both)


def exchange(both):
    return lax.all_to_all(both, TEAM, split_axis=0, concat_axis=0, tiled=True)


def dot(a, b, dims):
    return lax.dot_general(a, b, (dims, ((), ())), preferred_element_type=jnp.float32)


def attention_kernel(
    lists_ref,
    first_ref,
    kv_ref,
    qg_ref,
    prior_ref,
    sink_k_ref,
    sink_v_ref,
    seg_ref,
    out_ref,
    grads_ref,
    edges_ref,
    prior_out_ref,
    sink_out_ref,
    kx,
    vx,
    kt,
    vt,
    kt_far,
    vt_far,
    totals,
):
    step = pl.program_id(0)
    run = step // PER_RUN
    local = step % PER_RUN
    scale = 1.0 / math.sqrt(HD)

    @pl.when(step == 0)
    def _():
        for h in range(HEADS):
            at = slice(h * HD, (h + 1) * HD)
            kt_far[at] = sink_k_ref[:, at].T
            vt_far[at] = sink_v_ref[:, at].T
        sink_out_ref[...] = jnp.zeros_like(sink_out_ref)

    @pl.when(local == 0)
    def _():
        kx[:EDGE] = prior_ref[run, 0]
        vx[:EDGE] = prior_ref[run, 1]
        for h in range(HEADS):
            at = slice(h * HD, (h + 1) * HD)
            kt[at, :EDGE] = kx[:EDGE, at].T
            vt[at, :EDGE] = vx[:EDGE, at].T
        totals[:, :EDGE] = jnp.zeros((2, EDGE, COLS), jnp.float32)

    for n, x in ((0, kx), (1, vx)):
        for i in range(CHUNKS):
            x[EDGE + i * ROWS : EDGE + (i + 1) * ROWS] = kv_ref[i, n]

    key = lax.broadcasted_iota(jnp.int32, (BLK, BLK), 0)
    query = lax.broadcasted_iota(jnp.int32, (BLK, BLK), 1)

    def bias(ok):
        return jnp.where(ok, 0.0, NEG).astype(jnp.float32)

    masks = []
    for u in range(WORK):
        at_block = step * WORK + u
        here = first_ref[run] + local * WORK + u

        def listed(block, at_block=at_block):
            one = (lists_ref[at_block, 0] <= block) & (block < lists_ref[at_block, 1])
            two = (lists_ref[at_block, 2] <= block) & (block < lists_ref[at_block, 3])
            return one | two

        far = [bias(listed(i) & (i < here - REACH)) for i in range(SINK)]
        near = [here - REACH + i for i in range(REACH)]
        near = [bias(listed(x) & (x >= 0)) for x in near]
        seg_row = jnp.broadcast_to(seg_ref[pl.ds(at_block, 1), :], (BLK, BLK))
        order = (key <= query) | (seg_row == seg_row.T)
        masks.append(far + near + [jnp.where(order & listed(here), 0.0, NEG)])

    def blocks(x):
        return [x[i * BLK : (i + 1) * BLK] for i in range(x.shape[0] // BLK)]

    for h in range(HEADS):
        at = slice(h * HD, (h + 1) * HD)
        q_all = qg_ref[:, 0, :, at].reshape(WORK * BLK, HD)
        g_all = qg_ref[:, 1, :, at].reshape(WORK * BLK, HD)
        kt[at, EDGE:] = kx[EDGE:, at].T
        vt[at, EDGE:] = vx[EDGE:, at].T
        g_turned = g_all.astype(jnp.float32).T
        qs, gs = blocks(q_all), blocks(g_all)
        k_far, v_far = sink_k_ref[:, at], sink_v_ref[:, at]
        s_far = dot(k_far, q_all, ((1,), (1,)))
        dp_far = dot(v_far, g_all, ((1,), (1,)))
        ps, ws = [], []
        for u in range(WORK):
            lanes = slice(u * BLK, (u + 1) * BLK)
            span = slice(u * BLK, u * BLK + SPAN)
            s = blocks(s_far[:, lanes]) + blocks(dot(kx[span, at], qs[u], ((1,), (1,))))
            s = [x * (scale * LOG2E) + y for x, y in zip(s, masks[u])]
            top = jnp.max(functools.reduce(jnp.maximum, s), axis=0, keepdims=True)
            e = [jnp.exp2(x - top) for x in s]
            inv = 1.0 / jnp.sum(functools.reduce(jnp.add, e), axis=0, keepdims=True)
            p = [x * inv for x in e]
            ps.append(p)
            ws.append([x.astype(jnp.bfloat16) for x in p])
        w_far = jnp.concatenate([jnp.concatenate(w[:SINK], axis=0) for w in ws], axis=1)
        att_far = dot(vt_far[at, :], w_far, ((1,), (0,)))
        dss, atts = [], []
        for u in range(WORK):
            lanes = slice(u * BLK, (u + 1) * BLK)
            span = slice(u * BLK, u * BLK + SPAN)
            w_near = jnp.concatenate(ws[u][SINK:], axis=0)
            att = att_far[:, lanes] + dot(vt[at, span], w_near, ((1,), (0,)))
            att = att.astype(jnp.bfloat16).astype(jnp.float32)
            atts.append(att)
            delta = jnp.sum(g_turned[:, lanes] * att, axis=0, keepdims=True)
            dp = blocks(dp_far[:, lanes]) + blocks(dot(vx[span, at], gs[u], ((1,), (1,))))
            dss.append([(x * (y - delta)).astype(jnp.bfloat16) for x, y in zip(ps[u], dp)])
        ds_far = jnp.concatenate([jnp.concatenate(ds[:SINK], axis=0) for ds in dss], axis=1)
        dq_far = dot(kt_far[at, :], ds_far, ((1,), (0,)))
        dqs = []
        for u in range(WORK):
            lanes = slice(u * BLK, (u + 1) * BLK)
            span = slice(u * BLK, u * BLK + SPAN)
            ds_near = jnp.concatenate(dss[u][SINK:], axis=0)
            dqs.append(dq_far[:, lanes] + dot(kt[at, span], ds_near, ((1,), (0,))))
        att = jnp.concatenate(atts, axis=1).T.astype(jnp.bfloat16)
        dq = (scale * jnp.concatenate(dqs, axis=1)).T.astype(jnp.bfloat16)
        out_ref[:, 0, :, at] = att.reshape(CHUNKS, ROWS, HD)
        out_ref[:, 1, :, at] = dq.reshape(CHUNKS, ROWS, HD)
        sink_out_ref[0, :, at] += dot(ds_far, q_all, ((1,), (0,))) * scale
        sink_out_ref[1, :, at] += dot(w_far, g_all, ((1,), (0,)))
        for j in range(WORK + REACH):
            used = [u for u in range(WORK) if 0 <= j - u <= REACH]
            lanes = slice(used[0] * BLK, (used[-1] + 1) * BLK)
            ds = jnp.concatenate([dss[u][SINK + j - u] for u in used], axis=1)
            w = jnp.concatenate([ws[u][SINK + j - u] for u in used], axis=1)
            dk = dot(ds, q_all[lanes], ((1,), (0,))) * scale
            dv = dot(w, g_all[lanes], ((1,), (0,)))
            row = slice(j * BLK, (j + 1) * BLK)
            if j < REACH:
                totals[0, row, at] += dk
                totals[1, row, at] += dv
            else:
                totals[0, row, at] = dk
                totals[1, row, at] = dv

    lead = step * CHUNKS
    last = EDGE + BLK
    for n in range(2):
        body = totals[n, EDGE:last].astype(jnp.bfloat16)
        grads_ref[lead, n] = body[:ROWS]
        grads_ref[lead + 1, n, :REST] = body[ROWS:]

        @pl.when(local == 0)
        def _(n=n):
            prior_out_ref[run, n] = totals[n, :EDGE].astype(jnp.bfloat16)

        @pl.when(step == 0)
        def _(n=n):
            edges_ref[n, 0, :BLK] = totals[n, EDGE:last]

        @pl.when(step == 1)
        def _(n=n):
            edges_ref[n, 0, BLK:] = totals[n, :BLK]

        @pl.when(local > 0)
        def _(n=n):
            done = totals[n, :EDGE].astype(jnp.bfloat16)
            grads_ref[lead - 3, n, REST:] = done[:PART]
            grads_ref[lead - 2, n] = done[PART : PART + ROWS]
            grads_ref[lead - 1, n] = done[PART + ROWS :]

        @pl.when(local == PER_RUN - 1)
        def _(n=n):
            tail = totals[n, last:]
            edges_ref[n, 1 + run] = tail
            tail = tail.astype(jnp.bfloat16)
            grads_ref[lead + 1, n, REST:] = tail[:PART]
            grads_ref[lead + 2, n] = tail[PART : PART + ROWS]
            grads_ref[lead + 3, n] = tail[PART + ROWS :]

    kx[:EDGE] = kx[WORK * BLK :]
    vx[:EDGE] = vx[WORK * BLK :]
    kt[:, :EDGE] = kt[:, WORK * BLK :]
    vt[:, :EDGE] = vt[:, WORK * BLK :]
    totals[:, :EDGE] = totals[:, WORK * BLK :]


def attention(lists, first, kv, qg, prior, sink_k, sink_v, seg):
    def whole(shape):
        return pl.BlockSpec(shape, lambda i, *_: (0,) * len(shape))

    shapes = [
        jax.ShapeDtypeStruct((MEMBERS, 2, ROWS, COLS), jnp.bfloat16),
        jax.ShapeDtypeStruct((MEMBERS, 2, ROWS, COLS), jnp.bfloat16),
        jax.ShapeDtypeStruct((2, 1 + RUNS, EDGE, COLS), jnp.float32),
        jax.ShapeDtypeStruct((RUNS, 2, EDGE, COLS), jnp.bfloat16),
        jax.ShapeDtypeStruct((2, EDGE, COLS), jnp.float32),
    ]
    moving = pl.BlockSpec((CHUNKS, 2, ROWS, COLS), lambda i, *_: (i, 0, 0, 0))
    length = EDGE + WORK * BLK
    wide = pltpu.VMEM((length, COLS), jnp.bfloat16)
    turned = pltpu.VMEM((COLS, length), jnp.bfloat16)
    turned_far = pltpu.VMEM((COLS, EDGE), jnp.bfloat16)
    return pl.pallas_call(
        attention_kernel,
        grid_spec=pltpu.PrefetchScalarGridSpec(
            num_scalar_prefetch=2,
            grid=(STEPS,),
            in_specs=[moving, moving] + [whole(x.shape) for x in (prior, sink_k, sink_v, seg)],
            out_specs=[moving] + [whole(x.shape) for x in shapes[1:]],
            scratch_shapes=[
                wide,
                wide,
                turned,
                turned,
                turned_far,
                turned_far,
                pltpu.VMEM((2, length, COLS), jnp.float32),
            ],
        ),
        out_shape=shapes,
        compiler_params=params(),
        cost_estimate=pl.CostEstimate(flops=8000000000, bytes_accessed=16000000, transcendentals=3000000),
    )(lists, first, kv, qg, prior, sink_k, sink_v, seg)


def finish_kernel(owner_ref, grads_ref, edges_ref, back_ref, sink_ref, out_ref):
    keep = owner_ref[0].astype(jnp.float32)
    out_ref[...] = grads_ref[...]
    for n in range(2):
        head = (edges_ref[n, 0] + sink_ref[n] * keep).astype(jnp.bfloat16)
        out_ref[0, n] = head[:ROWS]
        out_ref[1, n] = head[ROWS : 2 * ROWS]
        out_ref[2, n, :PART] = head[2 * ROWS :]
        for run in range(RUNS):
            tail = edges_ref[n, 1 + run] + back_ref[run, n].astype(jnp.float32)
            tail = tail.astype(jnp.bfloat16)
            end = (run + 1) * RUN_CHUNKS
            out_ref[end - 3, n, REST:] = tail[:PART]
            out_ref[end - 2, n] = tail[PART : PART + ROWS]
            out_ref[end - 1, n] = tail[PART + ROWS :]


def finish(owner, grads, edges, back, sink):
    def whole(x):
        return pl.BlockSpec(x.shape, lambda i: (0,) * x.ndim)

    return pl.pallas_call(
        finish_kernel,
        grid=(1,),
        in_specs=[pl.BlockSpec(memory_space=pltpu.SMEM)] + [whole(x) for x in (grads, edges, back, sink)],
        out_specs=whole(grads),
        out_shape=jax.ShapeDtypeStruct(grads.shape, grads.dtype),
        compiler_params=params(),
        cost_estimate=pl.CostEstimate(flops=1000000, bytes_accessed=8000000, transcendentals=0),
    )(owner, grads, edges, back, sink)


def tie_kernel(value_ref, earlier_ref, out_ref):
    del value_ref, earlier_ref, out_ref


def tie(value, earlier):
    spec = pl.BlockSpec(memory_space=pl.ANY)
    return pl.pallas_call(
        tie_kernel,
        in_specs=[spec, spec],
        out_specs=spec,
        out_shape=jax.ShapeDtypeStruct(value.shape, value.dtype),
        input_output_aliases={0: 0},
        cost_estimate=pl.CostEstimate(flops=0, bytes_accessed=1024, transcendentals=0),
    )(value, earlier)


def send(value, pairs):
    return lax.ppermute(value, GROUPS, [(a * NZ + b, c * NZ + d) for (a, b), (c, d) in pairs])


EVERY = [(a, b) for a in range(NYO) for b in range(NZ)]
FORWARD = [((a, b), (a, (b + 1) % NZ)) for a, b in EVERY]
BACKWARD = [(b, a) for a, b in FORWARD]
TURN = [((0, NZ - 1), (1, 0))]
TURN_BACK = [((1, 0), (0, NZ - 1))]
ACROSS = [((0, 0), (1, 0))]
EVEN = [[((a, 0), (a, d)) for a in range(NYO)] for d in (2, 4, 6)]
ODD = [((a, b), (a, b + 1)) for a, b in EVERY if b % 2 == 0]
HOPS = [[ACROSS], EVEN, [ODD]]


def spread(value, hop, mine):
    got = functools.reduce(jnp.add, [send(value, pairs) for pairs in hop])
    return jnp.where(mine, value, got)


def collect(total, hop):
    sent = total.astype(jnp.bfloat16)
    got = [send(sent, [(b, a) for a, b in pairs]) for pairs in hop]
    return functools.reduce(jnp.add, [x.astype(jnp.float32) for x in got], total)


def swapped(value, axis):
    other = lax.ppermute(value, axis, [(0, 1), (1, 0)])
    first = lax.axis_index(axis) == 0
    return jnp.concatenate([jnp.where(first, value, other), jnp.where(first, other, value)])


def rows_of(both, start, stop, n):
    low, high = start // ROWS, -(-stop // ROWS)
    rows = both[low:high, n].reshape(-1, COLS)
    return rows[start - low * ROWS : stop - low * ROWS]


def per_device(queries, keys, values, grad_out, segment, lists):
    yo, z = lax.axis_index("yo"), lax.axis_index("z")
    small = jnp.concatenate([segment, lists.reshape(-1), jnp.zeros((116,), jnp.int32)])
    small = swapped(swapped(small.reshape(1, 512), "c"), "yi")
    seg = small[:, :384].reshape(BLOCKS, BLK).astype(jnp.float32)
    bounds = small[:, 384:396].reshape(BLOCKS, 4)

    kv = exchange(pack(keys, values))
    sinks = jnp.stack([rows_of(kv, 0, EDGE, n) for n in range(2)])
    sinks = spread(sinks, HOPS[0], yo == 0)
    run_rows = TOK // RUNS
    tails = [[rows_of(kv, r * run_rows - EDGE, r * run_rows, n) for n in range(2)] for r in (1, 2)]
    tails = [jnp.stack(x) for x in tails]
    came = send(jnp.stack(tails), FORWARD)
    turned = send(tails[1], TURN)
    prior = jnp.stack([jnp.where(z == 0, turned, came[0]), jnp.where(z == 0, came[0], came[1])])
    qg = exchange(tie(pack(queries, grad_out), sinks))
    sinks = spread(sinks, HOPS[1], z == 0)
    sinks = spread(sinks, HOPS[2], z % 2 == 0)

    starts = (jnp.arange(RUNS, dtype=jnp.int32) + yo * RUNS) * NZ + z
    first = starts * (BLOCKS // RUNS)
    out, grads, edges, prior_out, sink_out = attention(
        bounds, first, kv, qg, prior, sinks[0], sinks[1], seg
    )

    total = collect(sink_out, HOPS[2])
    went = send(prior_out, BACKWARD)
    turned = send(prior_out[0], TURN_BACK)
    back = jnp.stack([jnp.where(z == NZ - 1, went[1], went[0]), jnp.where(z == NZ - 1, turned, went[1])])
    out = exchange(tie(out, total))
    total = collect(total, HOPS[1])
    total = collect(total, HOPS[0])

    owner = ((yo == 0) & (z == 0)).astype(jnp.int32).reshape(1)
    grads = exchange(finish(owner, grads, edges, back, total))
    attended, grad_q = unpack(out)
    grad_k, grad_v = unpack(grads)
    return attended, grad_q, grad_k, grad_v


def solution(mesh):
    fine = Mesh(mesh.devices.reshape(NYO, 2, NZ, 2, 4), ("yo", "yi", "z", "c", "x"))
    ctx = ("yo", "yi", "z", "c")
    rows = P((*ctx, "x"), None)
    return jax.shard_map(
        per_device,
        mesh=fine,
        in_specs=(rows, rows, rows, rows, P(ctx), P(ctx, None, None)),
        out_specs=(rows, rows, rows, rows),
        check_vma=False,
    )
```

```python
import functools
import math

import jax
import jax.numpy as jnp
from jax import lax
from jax.experimental import pallas as pl
from jax.experimental.pallas import tpu as pltpu
from jax.sharding import Mesh
from jax.sharding import PartitionSpec as P

HD = 128
BLK = 128
REACH = 2
SINK = 2
NEG = -1e30
LOG2E = 1.4426950408889634

TEAM = ("yi", "c", "x")
GROUPS = ("yo", "z")
NYO, NZ = 2, 8
MEMBERS = 16
ROWS = 96
HEADS = 3
COLS = HEADS * HD
TOK = MEMBERS * ROWS
BLOCKS = TOK // BLK
RUNS = 2
EDGE = REACH * BLK
SPAN = EDGE + BLK
WORK = 3
STEPS = BLOCKS // WORK
PER_RUN = STEPS // RUNS
CHUNKS = WORK * BLK // ROWS
RUN_CHUNKS = MEMBERS // RUNS
PART = EDGE - 2 * ROWS
REST = ROWS - PART
PER = 8
VMEM = 56 * 1024 * 1024


def params():
    return pltpu.CompilerParams(vmem_limit_bytes=VMEM)


def pack_kernel(*refs):
    out_ref = refs[-1]
    for i in range(PER):
        for n, ref in enumerate(refs[:-1]):
            out_ref[i, n] = ref[:, i * COLS : (i + 1) * COLS]


def unpack_kernel(in_ref, *refs):
    for i in range(PER):
        for n, ref in enumerate(refs):
            ref[:, i * COLS : (i + 1) * COLS] = in_ref[i, n]


FLAT = pl.BlockSpec((ROWS, PER * COLS), lambda i: (0, i))


def stacked(count):
    return pl.BlockSpec((PER, count, ROWS, COLS), lambda i: (i, 0, 0, 0))


def stack_shape(count):
    return jax.ShapeDtypeStruct((MEMBERS, count, ROWS, COLS), jnp.bfloat16)


def cost(count):
    return pl.CostEstimate(flops=0, bytes_accessed=2400000 * count, transcendentals=0)


def pack(*values):
    count = len(values)
    return pl.pallas_call(
        pack_kernel,
        grid=(MEMBERS // PER,),
        in_specs=[FLAT] * count,
        out_specs=stacked(count),
        out_shape=stack_shape(count),
        compiler_params=params(),
        cost_estimate=cost(count),
    )(*values)


def unpack(both):
    count = both.shape[1]
    shape = jax.ShapeDtypeStruct((ROWS, MEMBERS * COLS), jnp.bfloat16)
    return pl.pallas_call(
        unpack_kernel,
        grid=(MEMBERS // PER,),
        in_specs=[stacked(count)],
        out_specs=[FLAT] * count,
        out_shape=[shape] * count,
        compiler_params=params(),
        cost_estimate=cost(count),
    )(both)


def exchange(both):
    return lax.all_to_all(both, TEAM, split_axis=0, concat_axis=0, tiled=True)


def dot(a, b, dims):
    return lax.dot_general(a, b, (dims, ((), ())), preferred_element_type=jnp.float32)


def window(step, prior_ref, kv_ref, kx, vx):
    run = step // PER_RUN

    @pl.when(step % PER_RUN == 0)
    def _():
        kx[:EDGE] = prior_ref[run, 0]
        vx[:EDGE] = prior_ref[run, 1]

    for n, x in ((0, kx), (1, vx)):
        for i in range(CHUNKS):
            x[EDGE + i * ROWS : EDGE + (i + 1) * ROWS] = kv_ref[i, n]


def masks_of(step, lists_ref, first_ref, seg_ref):
    run = step // PER_RUN
    local = step % PER_RUN
    key = lax.broadcasted_iota(jnp.int32, (BLK, BLK), 0)
    query = lax.broadcasted_iota(jnp.int32, (BLK, BLK), 1)

    def bias(ok):
        return jnp.where(ok, 0.0, NEG).astype(jnp.float32)

    masks = []
    for u in range(WORK):
        at_block = step * WORK + u
        here = first_ref[run] + local * WORK + u

        def listed(block, at_block=at_block):
            one = (lists_ref[at_block, 0] <= block) & (block < lists_ref[at_block, 1])
            two = (lists_ref[at_block, 2] <= block) & (block < lists_ref[at_block, 3])
            return one | two

        far = [bias(listed(i) & (i < here - REACH)) for i in range(SINK)]
        near = [here - REACH + i for i in range(REACH)]
        near = [bias(listed(x) & (x >= 0)) for x in near]
        seg_row = jnp.broadcast_to(seg_ref[pl.ds(at_block, 1), :], (BLK, BLK))
        order = (key <= query) | (seg_row == seg_row.T)
        masks.append(far + near + [jnp.where(order & listed(here), 0.0, NEG)])
    return masks


def blocks(x):
    return [x[i * BLK : (i + 1) * BLK] for i in range(x.shape[0] // BLK)]


def head_of(h):
    return slice(h * HD, (h + 1) * HD)


def lanes_of(u):
    return slice(u * BLK, (u + 1) * BLK)


def span_of(u):
    return slice(u * BLK, u * BLK + SPAN)


SCALE = 1.0 / math.sqrt(HD)


def forward_kernel(
    lists_ref,
    first_ref,
    kv_ref,
    g_ref,
    prior_ref,
    sink_k_ref,
    sink_v_ref,
    seg_ref,
    att_ref,
    lse_ref,
    delta_ref,
    dq_far_ref,
    sink_out_ref,
    sink_sent_ref,
    kx,
    vx,
    vt,
    kt_far,
    vt_far,
):
    step = pl.program_id(0)

    @pl.when(step == 0)
    def _():
        for h in range(HEADS):
            kt_far[head_of(h)] = sink_k_ref[:, head_of(h)].T
            vt_far[head_of(h)] = sink_v_ref[:, head_of(h)].T
        sink_out_ref[...] = jnp.zeros_like(sink_out_ref)

    window(step, prior_ref, kv_ref, kx, vx)
    masks = masks_of(step, lists_ref, first_ref, seg_ref)
    for h in range(HEADS):
        at = head_of(h)
        vt[at] = vx[:, at].T
        q_all = kv_ref[:, 2, :, at].reshape(WORK * BLK, HD)
        g_all = g_ref[:, 0, :, at].reshape(WORK * BLK, HD)
        qs = blocks(q_all)
        s_far = dot(sink_k_ref[:, at], q_all, ((1,), (1,)))
        dp_far = dot(sink_v_ref[:, at], g_all, ((1,), (1,)))
        ps, ws, logs = [], [], []
        for u in range(WORK):
            s = blocks(s_far[:, lanes_of(u)]) + blocks(dot(kx[span_of(u), at], qs[u], ((1,), (1,))))
            s = [x * (SCALE * LOG2E) + y for x, y in zip(s, masks[u])]
            top = jnp.max(functools.reduce(jnp.maximum, s), axis=0, keepdims=True)
            e = [jnp.exp2(x - top) for x in s]
            total = jnp.sum(functools.reduce(jnp.add, e), axis=0, keepdims=True)
            inv = 1.0 / total
            p = [x * inv for x in e]
            ps.append(jnp.concatenate(p[:SINK], axis=0))
            ws.append([x.astype(jnp.bfloat16) for x in p])
            logs.append(top + jnp.log(total) * LOG2E)
        w_far = jnp.concatenate([jnp.concatenate(w[:SINK], axis=0) for w in ws], axis=1)
        att_far = dot(vt_far[at, :], w_far, ((1,), (0,)))
        atts = []
        for u in range(WORK):
            w_near = jnp.concatenate(ws[u][SINK:], axis=0)
            atts.append(att_far[:, lanes_of(u)] + dot(vt[at, span_of(u)], w_near, ((1,), (0,))))
        att = jnp.concatenate(atts, axis=1).astype(jnp.bfloat16).astype(jnp.float32)
        delta = jnp.sum(g_all.astype(jnp.float32).T * att, axis=0, keepdims=True)
        ds_far = (jnp.concatenate(ps, axis=1) * (dp_far - delta)).astype(jnp.bfloat16)
        dq_far_ref[0, at] = dot(kt_far[at, :], ds_far, ((1,), (0,)))
        sink_out_ref[0, :, at] += dot(ds_far, q_all, ((1,), (0,))) * SCALE
        sink_out_ref[1, :, at] += dot(w_far, g_all, ((1,), (0,)))
        att_ref[:, 0, :, at] = att.T.astype(jnp.bfloat16).reshape(CHUNKS, ROWS, HD)
        lse_ref[0, h : h + 1, :] = jnp.concatenate(logs, axis=1)
        delta_ref[0, h : h + 1, :] = delta

    @pl.when(step == STEPS - 1)
    def _():
        sink_sent_ref[...] = sink_out_ref[...].astype(jnp.bfloat16)

    kx[:EDGE] = kx[WORK * BLK :]
    vx[:EDGE] = vx[WORK * BLK :]


def backward_kernel(
    lists_ref,
    first_ref,
    kv_ref,
    g_ref,
    lse_ref,
    delta_ref,
    dq_far_ref,
    att_ref,
    prior_ref,
    seg_ref,
    out_ref,
    grads_ref,
    edges_ref,
    prior_out_ref,
    kx,
    vx,
    kt,
    totals,
):
    step = pl.program_id(0)
    run = step // PER_RUN
    local = step % PER_RUN

    @pl.when(local == 0)
    def _():
        totals[:, :EDGE] = jnp.zeros((2, EDGE, COLS), jnp.float32)

    out_ref[:, 0] = att_ref[:, 0]
    window(step, prior_ref, kv_ref, kx, vx)
    masks = masks_of(step, lists_ref, first_ref, seg_ref)
    for h in range(HEADS):
        at = head_of(h)
        kt[at] = kx[:, at].T
        q_all = kv_ref[:, 2, :, at].reshape(WORK * BLK, HD)
        g_all = g_ref[:, 0, :, at].reshape(WORK * BLK, HD)
        lse = lse_ref[0, h : h + 1, :]
        delta = delta_ref[0, h : h + 1, :]
        dq_far = dq_far_ref[0, at]
        qs, gs = blocks(q_all), blocks(g_all)
        ws, dss = [], []
        for u in range(WORK):
            lanes, span = lanes_of(u), span_of(u)
            s = blocks(dot(kx[span, at], qs[u], ((1,), (1,))))
            dp = blocks(dot(vx[span, at], gs[u], ((1,), (1,))))
            near = masks[u][SINK:]
            p = [jnp.exp2(x * (SCALE * LOG2E) + y - lse[:, lanes]) for x, y in zip(s, near)]
            ws.append([x.astype(jnp.bfloat16) for x in p])
            dss.append([(x * (y - delta[:, lanes])).astype(jnp.bfloat16) for x, y in zip(p, dp)])
        dqs = []
        for u in range(WORK):
            ds_near = jnp.concatenate(dss[u], axis=0)
            dqs.append(dq_far[:, lanes_of(u)] + dot(kt[at, span_of(u)], ds_near, ((1,), (0,))))
        dq = (SCALE * jnp.concatenate(dqs, axis=1)).T.astype(jnp.bfloat16)
        out_ref[:, 1, :, at] = dq.reshape(CHUNKS, ROWS, HD)
        for j in range(WORK + REACH):
            used = [u for u in range(WORK) if 0 <= j - u <= REACH]
            lanes = slice(used[0] * BLK, (used[-1] + 1) * BLK)
            ds = jnp.concatenate([dss[u][j - u] for u in used], axis=1)
            w = jnp.concatenate([ws[u][j - u] for u in used], axis=1)
            dk = dot(ds, q_all[lanes], ((1,), (0,))) * SCALE
            dv = dot(w, g_all[lanes], ((1,), (0,)))
            row = slice(j * BLK, (j + 1) * BLK)
            if j < REACH:
                totals[0, row, at] += dk
                totals[1, row, at] += dv
            else:
                totals[0, row, at] = dk
                totals[1, row, at] = dv

    lead = step * CHUNKS
    last = EDGE + BLK
    for n in range(2):
        body = totals[n, EDGE:last].astype(jnp.bfloat16)
        grads_ref[lead, n] = body[:ROWS]
        grads_ref[lead + 1, n, :REST] = body[ROWS:]

        @pl.when(local == 0)
        def _(n=n):
            prior_out_ref[run, n] = totals[n, :EDGE].astype(jnp.bfloat16)

        @pl.when(step == 0)
        def _(n=n):
            edges_ref[n, 0, :BLK] = totals[n, EDGE:last]

        @pl.when(step == 1)
        def _(n=n):
            edges_ref[n, 0, BLK:] = totals[n, :BLK]

        @pl.when(local > 0)
        def _(n=n):
            done = totals[n, :EDGE].astype(jnp.bfloat16)
            grads_ref[lead - 3, n, REST:] = done[:PART]
            grads_ref[lead - 2, n] = done[PART : PART + ROWS]
            grads_ref[lead - 1, n] = done[PART + ROWS :]

        @pl.when(local == PER_RUN - 1)
        def _(n=n):
            tail = totals[n, last:]
            edges_ref[n, 1 + run] = tail
            tail = tail.astype(jnp.bfloat16)
            grads_ref[lead + 1, n, REST:] = tail[:PART]
            grads_ref[lead + 2, n] = tail[PART : PART + ROWS]
            grads_ref[lead + 3, n] = tail[PART + ROWS :]

    kx[:EDGE] = kx[WORK * BLK :]
    vx[:EDGE] = vx[WORK * BLK :]
    totals[:, :EDGE] = totals[:, WORK * BLK :]


LENGTH = EDGE + WORK * BLK
WIDE = pltpu.VMEM((LENGTH, COLS), jnp.bfloat16)
TURNED = pltpu.VMEM((COLS, LENGTH), jnp.bfloat16)
TURNED_FAR = pltpu.VMEM((COLS, EDGE), jnp.bfloat16)
LSE = jax.ShapeDtypeStruct((STEPS, HEADS, WORK * BLK), jnp.float32)
LSE_SPEC = pl.BlockSpec((1, HEADS, WORK * BLK), lambda i, *_: (i, 0, 0))


def whole(x):
    return pl.BlockSpec(x.shape, lambda i, *_: (0,) * len(x.shape))


def moving(count):
    return pl.BlockSpec((CHUNKS, count, ROWS, COLS), lambda i, *_: (i, 0, 0, 0))


DQ_FAR = jax.ShapeDtypeStruct((STEPS, COLS, WORK * BLK), jnp.float32)
DQ_FAR_SPEC = pl.BlockSpec((1, COLS, WORK * BLK), lambda i, *_: (i, 0, 0))


def forward(lists, first, kvq, g, prior, sink_k, sink_v, seg):
    sinks = [
        jax.ShapeDtypeStruct((2, EDGE, COLS), jnp.float32),
        jax.ShapeDtypeStruct((2, EDGE, COLS), jnp.bfloat16),
    ]
    return pl.pallas_call(
        forward_kernel,
        grid_spec=pltpu.PrefetchScalarGridSpec(
            num_scalar_prefetch=2,
            grid=(STEPS,),
            in_specs=[moving(3), moving(1)] + [whole(x) for x in (prior, sink_k, sink_v, seg)],
            out_specs=[moving(1), LSE_SPEC, LSE_SPEC, DQ_FAR_SPEC] + [whole(x) for x in sinks],
            scratch_shapes=[WIDE, WIDE, TURNED, TURNED_FAR, TURNED_FAR],
        ),
        out_shape=[stack_shape(1), LSE, LSE, DQ_FAR] + sinks,
        compiler_params=params(),
        cost_estimate=pl.CostEstimate(flops=6000000000, bytes_accessed=12000000, transcendentals=3000000),
    )(lists, first, kvq, g, prior, sink_k, sink_v, seg)


def backward(lists, first, kvq, g, lse, delta, dq_far, att, prior, seg):
    shapes = [
        stack_shape(2),
        stack_shape(2),
        jax.ShapeDtypeStruct((2, 1 + RUNS, EDGE, COLS), jnp.float32),
        jax.ShapeDtypeStruct((RUNS, 2, EDGE, COLS), jnp.bfloat16),
    ]
    return pl.pallas_call(
        backward_kernel,
        grid_spec=pltpu.PrefetchScalarGridSpec(
            num_scalar_prefetch=2,
            grid=(STEPS,),
            in_specs=[moving(3), moving(1), LSE_SPEC, LSE_SPEC, DQ_FAR_SPEC, moving(1)]
            + [whole(prior), whole(seg)],
            out_specs=[moving(2)] + [whole(x) for x in shapes[1:]],
            scratch_shapes=[WIDE, WIDE, TURNED, pltpu.VMEM((2, LENGTH, COLS), jnp.float32)],
        ),
        out_shape=shapes,
        compiler_params=params(),
        cost_estimate=pl.CostEstimate(flops=6000000000, bytes_accessed=16000000, transcendentals=2000000),
    )(lists, first, kvq, g, lse, delta, dq_far, att, prior, seg)


def put_rows(stage, out_ref, sems, first_chunk, aligned):
    cuts = (0, ROWS, 2 * ROWS, EDGE) if aligned else (0, PART, PART + ROWS, EDGE)
    copies = []
    for n in range(2):
        for i in range(3):
            low, high = cuts[i], cuts[i + 1]
            offset = 0 if aligned or i else REST
            copies.append(
                pltpu.make_async_copy(
                    stage.at[n, pl.ds(low, high - low)],
                    out_ref.at[first_chunk + i, n, pl.ds(offset, high - low)],
                    sems.at[n * 3 + i],
                )
            )
    return copies


def tails_kernel(grads_ref, edges_ref, back_ref, out_ref, stage, sems):
    del grads_ref
    copies = []
    for run in range(RUNS):
        for n in range(2):
            tail = edges_ref[n, 1 + run] + back_ref[run, n].astype(jnp.float32)
            stage[run, n] = tail.astype(jnp.bfloat16)
        first = (run + 1) * RUN_CHUNKS - 3
        copies += put_rows(stage.at[run], out_ref, sems.at[run], first, False)
    for copy in copies:
        copy.start()
    for copy in copies:
        copy.wait()


def head_kernel(owner_ref, grads_ref, edges_ref, total_ref, last_ref, out_ref, stage, sems):
    del grads_ref
    keep = owner_ref[0].astype(jnp.float32)
    for n in range(2):
        add = total_ref[n] + last_ref[n].astype(jnp.float32)
        stage[n] = (edges_ref[n, 0] + add * keep).astype(jnp.bfloat16)
    copies = put_rows(stage, out_ref, sems, 0, True)
    for copy in copies:
        copy.start()
    for copy in copies:
        copy.wait()


ANY = pl.BlockSpec(memory_space=pl.ANY)


def add_tails(grads, edges, back):
    return pl.pallas_call(
        tails_kernel,
        grid=(1,),
        in_specs=[ANY, whole(edges), whole(back)],
        out_specs=ANY,
        out_shape=jax.ShapeDtypeStruct(grads.shape, grads.dtype),
        scratch_shapes=[
            pltpu.VMEM((RUNS, 2, EDGE, COLS), jnp.bfloat16),
            pltpu.SemaphoreType.DMA((RUNS, 6)),
        ],
        input_output_aliases={0: 0},
        compiler_params=params(),
        cost_estimate=pl.CostEstimate(flops=1000000, bytes_accessed=4000000, transcendentals=0),
    )(grads, edges, back)


def add_head(owner, grads, edges, total, last):
    head = pl.BlockSpec((2, 1, EDGE, COLS), lambda i: (0, 0, 0, 0))
    return pl.pallas_call(
        head_kernel,
        grid=(1,),
        in_specs=[pl.BlockSpec(memory_space=pltpu.SMEM), ANY, head] + [whole(x) for x in (total, last)],
        out_specs=ANY,
        out_shape=jax.ShapeDtypeStruct(grads.shape, grads.dtype),
        scratch_shapes=[pltpu.VMEM((2, EDGE, COLS), jnp.bfloat16), pltpu.SemaphoreType.DMA((6,))],
        input_output_aliases={1: 0},
        compiler_params=params(),
        cost_estimate=pl.CostEstimate(flops=1000000, bytes_accessed=3000000, transcendentals=0),
    )(owner, grads, edges, total, last)


def tie_kernel(value_ref, earlier_ref, out_ref):
    del value_ref, earlier_ref, out_ref


def tie(value, earlier):
    spec = pl.BlockSpec(memory_space=pl.ANY)
    return pl.pallas_call(
        tie_kernel,
        in_specs=[spec, spec],
        out_specs=spec,
        out_shape=jax.ShapeDtypeStruct(value.shape, value.dtype),
        input_output_aliases={0: 0},
        cost_estimate=pl.CostEstimate(flops=0, bytes_accessed=1024, transcendentals=0),
    )(value, earlier)


def send(value, pairs):
    return lax.ppermute(value, GROUPS, [(a * NZ + b, c * NZ + d) for (a, b), (c, d) in pairs])


EVERY = [(a, b) for a in range(NYO) for b in range(NZ)]
FORWARD = [((a, b), (a, (b + 1) % NZ)) for a, b in EVERY]
BACKWARD = [(b, a) for a, b in FORWARD]
TURN = [((0, NZ - 1), (1, 0))]
TURN_BACK = [((1, 0), (0, NZ - 1))]
ACROSS = [((0, 0), (1, 0))]
EVEN = [[((a, 0), (a, d)) for a in range(NYO)] for d in (2, 4, 6)]
ODD = [((a, b), (a, b + 1)) for a, b in EVERY if b % 2 == 0]
HOPS = [[ACROSS], EVEN, [ODD]]


def spread(value, hop, mine):
    got = functools.reduce(jnp.add, [send(value, pairs) for pairs in hop])
    return jnp.where(mine, value, got)


def collect(total, hop, sent=None):
    sent = total.astype(jnp.bfloat16) if sent is None else sent
    got = [send(sent, [(b, a) for a, b in pairs]) for pairs in hop]
    return functools.reduce(jnp.add, [x.astype(jnp.float32) for x in got], total)


def gathered(value):
    names = ("yi", "c")
    pieces = [value] + [lax.ppermute(value, names, [(i, i ^ d) for i in range(4)]) for d in (1, 2, 3)]
    c_low, yi_low = lax.axis_index("c") == 0, lax.axis_index("yi") == 0
    a, b, c, d = pieces
    a, b, c, d = [jnp.where(c_low, m, n) for m, n in ((a, b), (b, a), (c, d), (d, c))]
    return jnp.concatenate([jnp.where(yi_low, m, n) for m, n in ((a, c), (b, d), (c, a), (d, b))])


def rows_of(both, start, stop, n):
    low, high = start // ROWS, -(-stop // ROWS)
    rows = both[low:high, n].reshape(-1, COLS)
    return rows[start - low * ROWS : stop - low * ROWS]


def per_device(queries, keys, values, grad_out, segment, lists):
    yo, z = lax.axis_index("yo"), lax.axis_index("z")
    small = jnp.concatenate([segment, lists.reshape(-1), jnp.zeros((116,), jnp.int32)])
    small = gathered(small.reshape(1, 512))
    seg = small[:, :384].reshape(BLOCKS, BLK).astype(jnp.float32)
    bounds = small[:, 384:396].reshape(BLOCKS, 4)

    kv = exchange(pack(keys, values, queries))
    sinks = jnp.stack([rows_of(kv, 0, EDGE, n) for n in range(2)])
    sinks = spread(sinks, HOPS[0], yo == 0)
    run_rows = TOK // RUNS
    tails = [[rows_of(kv, r * run_rows - EDGE, r * run_rows, n) for n in range(2)] for r in (1, 2)]
    tails = [jnp.stack(x) for x in tails]
    came = send(jnp.stack(tails), FORWARD)
    turned = send(tails[1], TURN)
    prior = jnp.stack([jnp.where(z == 0, turned, came[0]), jnp.where(z == 0, came[0], came[1])])
    g = exchange(tie(tie(pack(grad_out), prior), small))
    sinks = spread(sinks, HOPS[1], z == 0)
    sinks = spread(sinks, HOPS[2], z % 2 == 0)

    starts = (jnp.arange(RUNS, dtype=jnp.int32) + yo * RUNS) * NZ + z
    first = starts * (BLOCKS // RUNS)
    att, lse, delta, dq_far, sink_out, sink_sent = forward(
        bounds, first, kv, g, prior, sinks[0], sinks[1], seg
    )
    total = collect(sink_out, HOPS[2], sink_sent)
    out, grads, edges, prior_out = backward(
        bounds, first, kv, g, lse, delta, dq_far, att, prior, seg
    )
    out = exchange(tie(out, total))
    prior_out = tie(prior_out, total)

    went = send(prior_out, BACKWARD)
    turned = send(prior_out[0], TURN_BACK)
    back = jnp.stack([jnp.where(z == NZ - 1, went[1], went[0]), jnp.where(z == NZ - 1, turned, went[1])])
    total = collect(total, HOPS[1])
    last = send(total.astype(jnp.bfloat16), [(b, a) for a, b in ACROSS])

    owner = ((yo == 0) & (z == 0)).astype(jnp.int32).reshape(1)
    grads = add_tails(grads, edges, back)
    grads = exchange(add_head(owner, grads, edges, total, last))
    grad_k, grad_v = unpack(grads)
    attended, grad_q = unpack(out)
    return attended, grad_q, grad_k, grad_v


def solution(mesh):
    fine = Mesh(mesh.devices.reshape(NYO, 2, NZ, 2, 4), ("yo", "yi", "z", "c", "x"))
    ctx = ("yo", "yi", "z", "c")
    rows = P((*ctx, "x"), None)
    return jax.shard_map(
        per_device,
        mesh=fine,
        in_specs=(rows, rows, rows, rows, P(ctx), P(ctx, None, None)),
        out_specs=(rows, rows, rows, rows),
        check_vma=False,
    )
```

```python
import functools
import math

import jax
import jax.numpy as jnp
from jax import lax
from jax.experimental import pallas as pl
from jax.experimental.pallas import tpu as pltpu
from jax.sharding import Mesh
from jax.sharding import PartitionSpec as P

HD = 128
BLK = 128
REACH = 2
SINK = 2
NEG = -1e30
LOG2E = 1.4426950408889634

TEAM = ("yi", "c", "x")
GROUPS = ("yo", "z")
NYO, NZ = 2, 8
MEMBERS = 16
ROWS = 96
HEADS = 3
COLS = HEADS * HD
TOK = MEMBERS * ROWS
BLOCKS = TOK // BLK
RUNS = 2
EDGE = REACH * BLK
SPAN = EDGE + BLK
WORK = 3
STEPS = BLOCKS // WORK
PER_RUN = STEPS // RUNS
CHUNKS = WORK * BLK // ROWS
RUN_CHUNKS = MEMBERS // RUNS
PART = EDGE - 2 * ROWS
REST = ROWS - PART
PER = 8
VMEM = 56 * 1024 * 1024


def params():
    return pltpu.CompilerParams(vmem_limit_bytes=VMEM)


def pack_kernel(*refs):
    out_ref = refs[-1]
    for i in range(PER):
        for n, ref in enumerate(refs[:-1]):
            out_ref[i, n] = ref[:, i * COLS : (i + 1) * COLS]


def unpack_kernel(in_ref, *refs):
    for i in range(PER):
        for n, ref in enumerate(refs):
            ref[:, i * COLS : (i + 1) * COLS] = in_ref[i, n]


FLAT = pl.BlockSpec((ROWS, PER * COLS), lambda i: (0, i))


def stacked(count):
    return pl.BlockSpec((PER, count, ROWS, COLS), lambda i: (i, 0, 0, 0))


def stack_shape(count):
    return jax.ShapeDtypeStruct((MEMBERS, count, ROWS, COLS), jnp.bfloat16)


def cost(count):
    return pl.CostEstimate(flops=0, bytes_accessed=2400000 * count, transcendentals=0)


def pack(*values):
    count = len(values)
    return pl.pallas_call(
        pack_kernel,
        grid=(MEMBERS // PER,),
        in_specs=[FLAT] * count,
        out_specs=stacked(count),
        out_shape=stack_shape(count),
        compiler_params=params(),
        cost_estimate=cost(count),
    )(*values)


def unpack(both):
    count = both.shape[1]
    shape = jax.ShapeDtypeStruct((ROWS, MEMBERS * COLS), jnp.bfloat16)
    return pl.pallas_call(
        unpack_kernel,
        grid=(MEMBERS // PER,),
        in_specs=[stacked(count)],
        out_specs=[FLAT] * count,
        out_shape=[shape] * count,
        compiler_params=params(),
        cost_estimate=cost(count),
    )(both)


def exchange(both):
    return lax.all_to_all(both, TEAM, split_axis=0, concat_axis=0, tiled=True)


def dot(a, b, dims):
    return lax.dot_general(a, b, (dims, ((), ())), preferred_element_type=jnp.float32)


def window(step, prior_ref, kv_ref, kx, vx):
    run = step // PER_RUN

    @pl.when(step % PER_RUN == 0)
    def _():
        kx[:EDGE] = prior_ref[run, 0]
        vx[:EDGE] = prior_ref[run, 1]

    for n, x in ((0, kx), (1, vx)):
        for i in range(CHUNKS):
            x[EDGE + i * ROWS : EDGE + (i + 1) * ROWS] = kv_ref[i, n]


def masks_of(step, lists_ref, first_ref, seg_ref):
    run = step // PER_RUN
    local = step % PER_RUN
    key = lax.broadcasted_iota(jnp.int32, (BLK, BLK), 0)
    query = lax.broadcasted_iota(jnp.int32, (BLK, BLK), 1)

    def bias(ok):
        return jnp.where(ok, 0.0, NEG).astype(jnp.float32)

    masks = []
    for u in range(WORK):
        at_block = step * WORK + u
        here = first_ref[run] + local * WORK + u

        def listed(block, at_block=at_block):
            one = (lists_ref[at_block, 0] <= block) & (block < lists_ref[at_block, 1])
            two = (lists_ref[at_block, 2] <= block) & (block < lists_ref[at_block, 3])
            return one | two

        far = [bias(listed(i) & (i < here - REACH)) for i in range(SINK)]
        near = [here - REACH + i for i in range(REACH)]
        near = [bias(listed(x) & (x >= 0)) for x in near]
        seg_row = jnp.broadcast_to(seg_ref[pl.ds(at_block, 1), :], (BLK, BLK))
        order = (key <= query) | (seg_row == seg_row.T)
        masks.append(far + near + [jnp.where(order & listed(here), 0.0, NEG)])
    return masks


def blocks(x):
    return [x[i * BLK : (i + 1) * BLK] for i in range(x.shape[0] // BLK)]


def head_of(h):
    return slice(h * HD, (h + 1) * HD)


def lanes_of(u):
    return slice(u * BLK, (u + 1) * BLK)


def span_of(u):
    return slice(u * BLK, u * BLK + SPAN)


SCALE = 1.0 / math.sqrt(HD)


def forward_kernel(
    lists_ref,
    first_ref,
    kv_ref,
    g_ref,
    prior_ref,
    sink_k_ref,
    sink_v_ref,
    seg_ref,
    att_ref,
    lse_ref,
    delta_ref,
    dq_far_ref,
    sink_out_ref,
    sink_sent_ref,
    kx,
    vx,
    vt,
    kt_far,
    vt_far,
):
    step = pl.program_id(0)

    @pl.when(step == 0)
    def _():
        for h in range(HEADS):
            kt_far[head_of(h)] = sink_k_ref[:, head_of(h)].T
            vt_far[head_of(h)] = sink_v_ref[:, head_of(h)].T
        sink_out_ref[...] = jnp.zeros_like(sink_out_ref)

    window(step, prior_ref, kv_ref, kx, vx)
    masks = masks_of(step, lists_ref, first_ref, seg_ref)
    for h in range(HEADS):
        at = head_of(h)
        vt[at] = vx[:, at].T
        q_all = kv_ref[:, 2, :, at].reshape(WORK * BLK, HD)
        g_all = g_ref[:, 0, :, at].reshape(WORK * BLK, HD)
        qs = blocks(q_all)
        s_far = dot(sink_k_ref[:, at], q_all, ((1,), (1,)))
        dp_far = dot(sink_v_ref[:, at], g_all, ((1,), (1,)))
        ps, ws, logs = [], [], []
        for u in range(WORK):
            s = blocks(s_far[:, lanes_of(u)]) + blocks(dot(kx[span_of(u), at], qs[u], ((1,), (1,))))
            s = [x * (SCALE * LOG2E) + y for x, y in zip(s, masks[u])]
            top = jnp.max(functools.reduce(jnp.maximum, s), axis=0, keepdims=True)
            e = [jnp.exp2(x - top) for x in s]
            total = jnp.sum(functools.reduce(jnp.add, e), axis=0, keepdims=True)
            inv = 1.0 / total
            p = [x * inv for x in e]
            ps.append(jnp.concatenate(p[:SINK], axis=0))
            ws.append([x.astype(jnp.bfloat16) for x in p])
            logs.append(top + jnp.log(total) * LOG2E)
        w_far = jnp.concatenate([jnp.concatenate(w[:SINK], axis=0) for w in ws], axis=1)
        att_far = dot(vt_far[at, :], w_far, ((1,), (0,)))
        atts = []
        for u in range(WORK):
            w_near = jnp.concatenate(ws[u][SINK:], axis=0)
            atts.append(att_far[:, lanes_of(u)] + dot(vt[at, span_of(u)], w_near, ((1,), (0,))))
        att = jnp.concatenate(atts, axis=1).astype(jnp.bfloat16).astype(jnp.float32)
        delta = jnp.sum(g_all.astype(jnp.float32).T * att, axis=0, keepdims=True)
        ds_far = (jnp.concatenate(ps, axis=1) * (dp_far - delta)).astype(jnp.bfloat16)
        dq_far_ref[0, at] = dot(kt_far[at, :], ds_far, ((1,), (0,)))
        sink_out_ref[0, :, at] += dot(ds_far, q_all, ((1,), (0,))) * SCALE
        sink_out_ref[1, :, at] += dot(w_far, g_all, ((1,), (0,)))
        att_ref[:, 0, :, at] = att.T.astype(jnp.bfloat16).reshape(CHUNKS, ROWS, HD)
        lse_ref[0, h : h + 1, :] = jnp.concatenate(logs, axis=1)
        delta_ref[0, h : h + 1, :] = delta

    @pl.when(step == STEPS - 1)
    def _():
        sink_sent_ref[...] = sink_out_ref[...].astype(jnp.bfloat16)

    kx[:EDGE] = kx[WORK * BLK :]
    vx[:EDGE] = vx[WORK * BLK :]


def backward_kernel(
    lists_ref,
    first_ref,
    kv_ref,
    g_ref,
    lse_ref,
    delta_ref,
    dq_far_ref,
    att_ref,
    prior_ref,
    seg_ref,
    out_ref,
    grads_ref,
    edges_ref,
    prior_out_ref,
    kx,
    vx,
    kt,
    totals,
):
    step = pl.program_id(0)
    run = step // PER_RUN
    local = step % PER_RUN

    @pl.when(local == 0)
    def _():
        totals[:, :EDGE] = jnp.zeros((2, EDGE, COLS), jnp.float32)

    out_ref[:, 0] = att_ref[:, 0]
    window(step, prior_ref, kv_ref, kx, vx)
    masks = masks_of(step, lists_ref, first_ref, seg_ref)
    for h in range(HEADS):
        at = head_of(h)
        kt[at] = kx[:, at].T
        q_all = kv_ref[:, 2, :, at].reshape(WORK * BLK, HD)
        g_all = g_ref[:, 0, :, at].reshape(WORK * BLK, HD)
        lse = lse_ref[0, h : h + 1, :]
        delta = delta_ref[0, h : h + 1, :]
        dq_far = dq_far_ref[0, at]
        qs, gs = blocks(q_all), blocks(g_all)
        ws, dss = [], []
        for u in range(WORK):
            lanes, span = lanes_of(u), span_of(u)
            s = blocks(dot(kx[span, at], qs[u], ((1,), (1,))))
            dp = blocks(dot(vx[span, at], gs[u], ((1,), (1,))))
            near = masks[u][SINK:]
            p = [jnp.exp2(x * (SCALE * LOG2E) + y - lse[:, lanes]) for x, y in zip(s, near)]
            ws.append([x.astype(jnp.bfloat16) for x in p])
            dss.append([(x * (y - delta[:, lanes])).astype(jnp.bfloat16) for x, y in zip(p, dp)])
        dqs = []
        for u in range(WORK):
            ds_near = jnp.concatenate(dss[u], axis=0)
            dqs.append(dq_far[:, lanes_of(u)] + dot(kt[at, span_of(u)], ds_near, ((1,), (0,))))
        dq = (SCALE * jnp.concatenate(dqs, axis=1)).T.astype(jnp.bfloat16)
        out_ref[:, 1, :, at] = dq.reshape(CHUNKS, ROWS, HD)
        for j in range(WORK + REACH):
            used = [u for u in range(WORK) if 0 <= j - u <= REACH]
            lanes = slice(used[0] * BLK, (used[-1] + 1) * BLK)
            ds = jnp.concatenate([dss[u][j - u] for u in used], axis=1)
            w = jnp.concatenate([ws[u][j - u] for u in used], axis=1)
            dk = dot(ds, q_all[lanes], ((1,), (0,))) * SCALE
            dv = dot(w, g_all[lanes], ((1,), (0,)))
            row = slice(j * BLK, (j + 1) * BLK)
            if j < REACH:
                totals[0, row, at] += dk
                totals[1, row, at] += dv
            else:
                totals[0, row, at] = dk
                totals[1, row, at] = dv

    lead = step * CHUNKS
    last = EDGE + BLK
    for n in range(2):
        body = totals[n, EDGE:last].astype(jnp.bfloat16)
        grads_ref[lead, n] = body[:ROWS]
        grads_ref[lead + 1, n, :REST] = body[ROWS:]

        @pl.when(local == 0)
        def _(n=n):
            prior_out_ref[run, n] = totals[n, :EDGE].astype(jnp.bfloat16)

        @pl.when(step == 0)
        def _(n=n):
            edges_ref[n, 0, :BLK] = totals[n, EDGE:last]

        @pl.when(step == 1)
        def _(n=n):
            edges_ref[n, 0, BLK:] = totals[n, :BLK]

        @pl.when(local > 0)
        def _(n=n):
            done = totals[n, :EDGE].astype(jnp.bfloat16)
            grads_ref[lead - 3, n, REST:] = done[:PART]
            grads_ref[lead - 2, n] = done[PART : PART + ROWS]
            grads_ref[lead - 1, n] = done[PART + ROWS :]

        @pl.when(local == PER_RUN - 1)
        def _(n=n):
            tail = totals[n, last:]
            edges_ref[n, 1 + run] = tail
            tail = tail.astype(jnp.bfloat16)
            grads_ref[lead + 1, n, REST:] = tail[:PART]
            grads_ref[lead + 2, n] = tail[PART : PART + ROWS]
            grads_ref[lead + 3, n] = tail[PART + ROWS :]

    kx[:EDGE] = kx[WORK * BLK :]
    vx[:EDGE] = vx[WORK * BLK :]
    totals[:, :EDGE] = totals[:, WORK * BLK :]


LENGTH = EDGE + WORK * BLK
WIDE = pltpu.VMEM((LENGTH, COLS), jnp.bfloat16)
TURNED = pltpu.VMEM((COLS, LENGTH), jnp.bfloat16)
TURNED_FAR = pltpu.VMEM((COLS, EDGE), jnp.bfloat16)
LSE = jax.ShapeDtypeStruct((STEPS, HEADS, WORK * BLK), jnp.float32)
LSE_SPEC = pl.BlockSpec((1, HEADS, WORK * BLK), lambda i, *_: (i, 0, 0))


def whole(x):
    return pl.BlockSpec(x.shape, lambda i, *_: (0,) * len(x.shape))


def moving(count):
    return pl.BlockSpec((CHUNKS, count, ROWS, COLS), lambda i, *_: (i, 0, 0, 0))


DQ_FAR = jax.ShapeDtypeStruct((STEPS, COLS, WORK * BLK), jnp.float32)
DQ_FAR_SPEC = pl.BlockSpec((1, COLS, WORK * BLK), lambda i, *_: (i, 0, 0))


def forward(lists, first, kvq, g, prior, sink_k, sink_v, seg):
    sinks = [
        jax.ShapeDtypeStruct((2, EDGE, COLS), jnp.float32),
        jax.ShapeDtypeStruct((2, EDGE, COLS), jnp.bfloat16),
    ]
    return pl.pallas_call(
        forward_kernel,
        grid_spec=pltpu.PrefetchScalarGridSpec(
            num_scalar_prefetch=2,
            grid=(STEPS,),
            in_specs=[moving(3), moving(1)] + [whole(x) for x in (prior, sink_k, sink_v, seg)],
            out_specs=[moving(1), LSE_SPEC, LSE_SPEC, DQ_FAR_SPEC] + [whole(x) for x in sinks],
            scratch_shapes=[WIDE, WIDE, TURNED, TURNED_FAR, TURNED_FAR],
        ),
        out_shape=[stack_shape(1), LSE, LSE, DQ_FAR] + sinks,
        compiler_params=params(),
        cost_estimate=pl.CostEstimate(flops=6000000000, bytes_accessed=12000000, transcendentals=3000000),
    )(lists, first, kvq, g, prior, sink_k, sink_v, seg)


def backward(lists, first, kvq, g, lse, delta, dq_far, att, prior, seg):
    shapes = [
        stack_shape(2),
        stack_shape(2),
        jax.ShapeDtypeStruct((2, 1 + RUNS, EDGE, COLS), jnp.float32),
        jax.ShapeDtypeStruct((RUNS, 2, EDGE, COLS), jnp.bfloat16),
    ]
    return pl.pallas_call(
        backward_kernel,
        grid_spec=pltpu.PrefetchScalarGridSpec(
            num_scalar_prefetch=2,
            grid=(STEPS,),
            in_specs=[moving(3), moving(1), LSE_SPEC, LSE_SPEC, DQ_FAR_SPEC, moving(1)]
            + [whole(prior), whole(seg)],
            out_specs=[moving(2)] + [whole(x) for x in shapes[1:]],
            scratch_shapes=[WIDE, WIDE, TURNED, pltpu.VMEM((2, LENGTH, COLS), jnp.float32)],
        ),
        out_shape=shapes,
        compiler_params=params(),
        cost_estimate=pl.CostEstimate(flops=6000000000, bytes_accessed=16000000, transcendentals=2000000),
    )(lists, first, kvq, g, lse, delta, dq_far, att, prior, seg)


def put_rows(stage, out_ref, sems, first_chunk, aligned):
    cuts = (0, ROWS, 2 * ROWS, EDGE) if aligned else (0, PART, PART + ROWS, EDGE)
    copies = []
    for n in range(2):
        for i in range(3):
            low, high = cuts[i], cuts[i + 1]
            offset = 0 if aligned or i else REST
            copies.append(
                pltpu.make_async_copy(
                    stage.at[n, pl.ds(low, high - low)],
                    out_ref.at[first_chunk + i, n, pl.ds(offset, high - low)],
                    sems.at[n * 3 + i],
                )
            )
    return copies


def tails_kernel(grads_ref, edges_ref, back_ref, out_ref, stage, sems):
    del grads_ref
    copies = []
    for run in range(RUNS):
        for n in range(2):
            tail = edges_ref[n, 1 + run] + back_ref[run, n].astype(jnp.float32)
            stage[run, n] = tail.astype(jnp.bfloat16)
        first = (run + 1) * RUN_CHUNKS - 3
        copies += put_rows(stage.at[run], out_ref, sems.at[run], first, False)
    for copy in copies:
        copy.start()
    for copy in copies:
        copy.wait()


def head_kernel(owner_ref, grads_ref, edges_ref, total_ref, last_ref, out_ref, stage, sems):
    del grads_ref
    keep = owner_ref[0].astype(jnp.float32)
    for n in range(2):
        add = total_ref[n] + last_ref[n].astype(jnp.float32)
        stage[n] = (edges_ref[n, 0] + add * keep).astype(jnp.bfloat16)
    copies = put_rows(stage, out_ref, sems, 0, True)
    for copy in copies:
        copy.start()
    for copy in copies:
        copy.wait()


ANY = pl.BlockSpec(memory_space=pl.ANY)


def add_tails(grads, edges, back):
    return pl.pallas_call(
        tails_kernel,
        grid=(1,),
        in_specs=[ANY, whole(edges), whole(back)],
        out_specs=ANY,
        out_shape=jax.ShapeDtypeStruct(grads.shape, grads.dtype),
        scratch_shapes=[
            pltpu.VMEM((RUNS, 2, EDGE, COLS), jnp.bfloat16),
            pltpu.SemaphoreType.DMA((RUNS, 6)),
        ],
        input_output_aliases={0: 0},
        compiler_params=params(),
        cost_estimate=pl.CostEstimate(flops=1000000, bytes_accessed=4000000, transcendentals=0),
    )(grads, edges, back)


def add_head(owner, grads, edges, total, last):
    head = pl.BlockSpec((2, 1, EDGE, COLS), lambda i: (0, 0, 0, 0))
    return pl.pallas_call(
        head_kernel,
        grid=(1,),
        in_specs=[pl.BlockSpec(memory_space=pltpu.SMEM), ANY, head] + [whole(x) for x in (total, last)],
        out_specs=ANY,
        out_shape=jax.ShapeDtypeStruct(grads.shape, grads.dtype),
        scratch_shapes=[pltpu.VMEM((2, EDGE, COLS), jnp.bfloat16), pltpu.SemaphoreType.DMA((6,))],
        input_output_aliases={1: 0},
        compiler_params=params(),
        cost_estimate=pl.CostEstimate(flops=1000000, bytes_accessed=3000000, transcendentals=0),
    )(owner, grads, edges, total, last)


def tie_kernel(value_ref, earlier_ref, out_ref):
    del value_ref, earlier_ref, out_ref


def tie(value, earlier):
    spec = pl.BlockSpec(memory_space=pl.ANY)
    return pl.pallas_call(
        tie_kernel,
        in_specs=[spec, spec],
        out_specs=spec,
        out_shape=jax.ShapeDtypeStruct(value.shape, value.dtype),
        input_output_aliases={0: 0},
        cost_estimate=pl.CostEstimate(flops=0, bytes_accessed=1024, transcendentals=0),
    )(value, earlier)


def send(value, pairs):
    return lax.ppermute(value, GROUPS, [(a * NZ + b, c * NZ + d) for (a, b), (c, d) in pairs])


EVERY = [(a, b) for a in range(NYO) for b in range(NZ)]
FORWARD = [((a, b), (a, (b + 1) % NZ)) for a, b in EVERY]
BACKWARD = [(b, a) for a, b in FORWARD]
TURN = [((0, NZ - 1), (1, 0))]
TURN_BACK = [((1, 0), (0, NZ - 1))]
ACROSS = [((0, 0), (1, 0))]
EVEN = [[((a, 0), (a, d)) for a in range(NYO)] for d in (2, 4, 6)]
ODD = [((a, b), (a, b + 1)) for a, b in EVERY if b % 2 == 0]
HOPS = [[ACROSS], EVEN, [ODD]]


def spread(value, hop, mine):
    got = functools.reduce(jnp.add, [send(value, pairs) for pairs in hop])
    return jnp.where(mine, value, got)


def collect(total, hop, sent=None):
    sent = total.astype(jnp.bfloat16) if sent is None else sent
    got = [send(sent, [(b, a) for a, b in pairs]) for pairs in hop]
    return functools.reduce(jnp.add, [x.astype(jnp.float32) for x in got], total)


def gathered(value):
    names = ("yi", "c")
    pieces = [value] + [lax.ppermute(value, names, [(i, i ^ d) for i in range(4)]) for d in (1, 2, 3)]
    c_low, yi_low = lax.axis_index("c") == 0, lax.axis_index("yi") == 0
    a, b, c, d = pieces
    a, b, c, d = [jnp.where(c_low, m, n) for m, n in ((a, b), (b, a), (c, d), (d, c))]
    return jnp.concatenate([jnp.where(yi_low, m, n) for m, n in ((a, c), (b, d), (c, a), (d, b))])


def rows_of(both, start, stop, n):
    low, high = start // ROWS, -(-stop // ROWS)
    rows = both[low:high, n].reshape(-1, COLS)
    return rows[start - low * ROWS : stop - low * ROWS]


def per_device(queries, keys, values, grad_out, segment, lists):
    yo, z = lax.axis_index("yo"), lax.axis_index("z")
    small = jnp.concatenate([segment, lists.reshape(-1), jnp.zeros((116,), jnp.int32)])
    small = gathered(small.reshape(1, 512))
    seg = small[:, :384].reshape(BLOCKS, BLK).astype(jnp.float32)
    bounds = small[:, 384:396].reshape(BLOCKS, 4)

    kv = exchange(pack(keys, values, queries))
    sinks = jnp.stack([rows_of(kv, 0, EDGE, n) for n in range(2)])
    sinks = spread(sinks, HOPS[0], yo == 0)
    run_rows = TOK // RUNS
    tails = [[rows_of(kv, r * run_rows - EDGE, r * run_rows, n) for n in range(2)] for r in (1, 2)]
    tails = [jnp.stack(x) for x in tails]
    came = send(jnp.stack(tails), FORWARD)
    turned = send(tails[1], TURN)
    prior = jnp.stack([jnp.where(z == 0, turned, came[0]), jnp.where(z == 0, came[0], came[1])])
    g = exchange(tie(pack(grad_out), prior))
    sinks = spread(sinks, HOPS[1], z == 0)
    sinks = spread(sinks, HOPS[2], z % 2 == 0)

    starts = (jnp.arange(RUNS, dtype=jnp.int32) + yo * RUNS) * NZ + z
    first = starts * (BLOCKS // RUNS)
    att, lse, delta, dq_far, sink_out, sink_sent = forward(
        bounds, first, kv, g, prior, sinks[0], sinks[1], seg
    )
    total = collect(sink_out, HOPS[2], sink_sent)
    out, grads, edges, prior_out = backward(
        bounds, first, kv, g, lse, delta, dq_far, att, prior, seg
    )
    out = exchange(tie(out, total))
    prior_out = tie(prior_out, total)

    went = send(prior_out, BACKWARD)
    turned = send(prior_out[0], TURN_BACK)
    back = jnp.stack([jnp.where(z == NZ - 1, went[1], went[0]), jnp.where(z == NZ - 1, turned, went[1])])
    total = collect(total, HOPS[1])
    last = send(total.astype(jnp.bfloat16), [(b, a) for a, b in ACROSS])

    owner = ((yo == 0) & (z == 0)).astype(jnp.int32).reshape(1)
    grads = add_tails(grads, edges, back)
    grads = exchange(add_head(owner, grads, edges, total, last))
    grad_k, grad_v = unpack(grads)
    attended, grad_q = unpack(out)
    return attended, grad_q, grad_k, grad_v


def solution(mesh):
    fine = Mesh(mesh.devices.reshape(NYO, 2, NZ, 2, 4), ("yo", "yi", "z", "c", "x"))
    ctx = ("yo", "yi", "z", "c")
    rows = P((*ctx, "x"), None)
    return jax.shard_map(
        per_device,
        mesh=fine,
        in_specs=(rows, rows, rows, rows, P(ctx), P(ctx, None, None)),
        out_specs=(rows, rows, rows, rows),
        check_vma=False,
    )
```

```python
import functools
import math

import jax
import jax.numpy as jnp
from jax import lax
from jax.experimental import pallas as pl
from jax.experimental.pallas import tpu as pltpu
from jax.sharding import Mesh
from jax.sharding import PartitionSpec as P

HD = 128
BLK = 128
REACH = 2
SINK = 2
NEG = -1e30
LOG2E = 1.4426950408889634

TEAM = ("yi", "c", "x")
GROUPS = ("yo", "z")
NYO, NZ = 2, 8
MEMBERS = 16
ROWS = 96
HEADS = 3
COLS = HEADS * HD
TOK = MEMBERS * ROWS
BLOCKS = TOK // BLK
RUNS = 2
EDGE = REACH * BLK
SPAN = EDGE + BLK
WORK = 3
STEPS = BLOCKS // WORK
PER_RUN = STEPS // RUNS
CHUNKS = WORK * BLK // ROWS
RUN_CHUNKS = MEMBERS // RUNS
PART = EDGE - 2 * ROWS
REST = ROWS - PART
PER = 8
VMEM = 62 * 1024 * 1024


def params():
    return pltpu.CompilerParams(vmem_limit_bytes=VMEM)


def pack_kernel(*refs):
    out_ref = refs[-1]
    for i in range(PER):
        for n, ref in enumerate(refs[:-1]):
            out_ref[i, n] = ref[:, i * COLS : (i + 1) * COLS]


def unpack_kernel(in_ref, *refs):
    for i in range(PER):
        for n, ref in enumerate(refs):
            ref[:, i * COLS : (i + 1) * COLS] = in_ref[i, n]


FLAT = pl.BlockSpec((ROWS, PER * COLS), lambda i: (0, i))


def stacked(count):
    return pl.BlockSpec((PER, count, ROWS, COLS), lambda i: (i, 0, 0, 0))


def stack_shape(count):
    return jax.ShapeDtypeStruct((MEMBERS, count, ROWS, COLS), jnp.bfloat16)


def cost(count):
    return pl.CostEstimate(flops=0, bytes_accessed=2400000 * count, transcendentals=0)


def pack(*values):
    count = len(values)
    return pl.pallas_call(
        pack_kernel,
        grid=(MEMBERS // PER,),
        in_specs=[FLAT] * count,
        out_specs=stacked(count),
        out_shape=stack_shape(count),
        compiler_params=params(),
        cost_estimate=cost(count),
    )(*values)


def unpack(both):
    count = both.shape[1]
    shape = jax.ShapeDtypeStruct((ROWS, MEMBERS * COLS), jnp.bfloat16)
    return pl.pallas_call(
        unpack_kernel,
        grid=(MEMBERS // PER,),
        in_specs=[stacked(count)],
        out_specs=[FLAT] * count,
        out_shape=[shape] * count,
        compiler_params=params(),
        cost_estimate=cost(count),
    )(both)


def exchange(both):
    return lax.all_to_all(both, TEAM, split_axis=0, concat_axis=0, tiled=True)


def dot(a, b, dims):
    return lax.dot_general(a, b, (dims, ((), ())), preferred_element_type=jnp.float32)


def window(step, prior_ref, kv_ref, kx, vx):
    run = step // PER_RUN

    @pl.when(step % PER_RUN == 0)
    def _():
        kx[:EDGE] = prior_ref[run, 0]
        vx[:EDGE] = prior_ref[run, 1]

    for n, x in ((0, kx), (1, vx)):
        for i in range(CHUNKS):
            x[EDGE + i * ROWS : EDGE + (i + 1) * ROWS] = kv_ref[i, n]


def masks_of(step, lists_ref, first_ref, seg_ref):
    run = step // PER_RUN
    local = step % PER_RUN
    key = lax.broadcasted_iota(jnp.int32, (BLK, BLK), 0)
    query = lax.broadcasted_iota(jnp.int32, (BLK, BLK), 1)

    def bias(ok):
        return jnp.where(ok, 0.0, NEG).astype(jnp.float32)

    masks = []
    for u in range(WORK):
        at_block = step * WORK + u
        here = first_ref[run] + local * WORK + u

        def listed(block, at_block=at_block):
            one = (lists_ref[at_block, 0] <= block) & (block < lists_ref[at_block, 1])
            two = (lists_ref[at_block, 2] <= block) & (block < lists_ref[at_block, 3])
            return one | two

        far = [bias(listed(i) & (i < here - REACH)) for i in range(SINK)]
        near = [here - REACH + i for i in range(REACH)]
        near = [bias(listed(x) & (x >= 0)) for x in near]
        seg_row = jnp.broadcast_to(seg_ref[pl.ds(at_block, 1), :], (BLK, BLK))
        order = (key <= query) | (seg_row == seg_row.T)
        masks.append(far + near + [jnp.where(order & listed(here), 0.0, NEG)])
    return masks


def blocks(x):
    return [x[i * BLK : (i + 1) * BLK] for i in range(x.shape[0] // BLK)]


def head_of(h):
    return slice(h * HD, (h + 1) * HD)


def lanes_of(u):
    return slice(u * BLK, (u + 1) * BLK)


def span_of(u):
    return slice(u * BLK, u * BLK + SPAN)


SCALE = 1.0 / math.sqrt(HD)


def forward_kernel(
    lists_ref,
    first_ref,
    kv_ref,
    g_ref,
    prior_ref,
    sink_k_ref,
    sink_v_ref,
    seg_ref,
    att_ref,
    lse_ref,
    delta_ref,
    dq_far_ref,
    sink_out_ref,
    sink_sent_ref,
    kx,
    vx,
    vt,
    kt_far,
    vt_far,
):
    step = pl.program_id(0)

    @pl.when(step == 0)
    def _():
        for h in range(HEADS):
            kt_far[head_of(h)] = sink_k_ref[:, head_of(h)].T
            vt_far[head_of(h)] = sink_v_ref[:, head_of(h)].T
        sink_out_ref[...] = jnp.zeros_like(sink_out_ref)

    window(step, prior_ref, kv_ref, kx, vx)
    masks = masks_of(step, lists_ref, first_ref, seg_ref)
    for h in range(HEADS):
        at = head_of(h)
        vt[at] = vx[:, at].T
        q_all = kv_ref[:, 2, :, at].reshape(WORK * BLK, HD)
        g_all = g_ref[:, 0, :, at].reshape(WORK * BLK, HD)
        qs = blocks(q_all)
        s_far = dot(sink_k_ref[:, at], q_all, ((1,), (1,)))
        dp_far = dot(sink_v_ref[:, at], g_all, ((1,), (1,)))
        ps, ws, logs = [], [], []
        for u in range(WORK):
            s = blocks(s_far[:, lanes_of(u)]) + blocks(dot(kx[span_of(u), at], qs[u], ((1,), (1,))))
            s = [x * (SCALE * LOG2E) + y for x, y in zip(s, masks[u])]
            top = jnp.max(functools.reduce(jnp.maximum, s), axis=0, keepdims=True)
            e = [jnp.exp2(x - top) for x in s]
            total = jnp.sum(functools.reduce(jnp.add, e), axis=0, keepdims=True)
            inv = 1.0 / total
            p = [x * inv for x in e]
            ps.append(jnp.concatenate(p[:SINK], axis=0))
            ws.append([x.astype(jnp.bfloat16) for x in p])
            logs.append(top + jnp.log(total) * LOG2E)
        w_far = jnp.concatenate([jnp.concatenate(w[:SINK], axis=0) for w in ws], axis=1)
        att_far = dot(vt_far[at, :], w_far, ((1,), (0,)))
        atts = []
        for u in range(WORK):
            w_near = jnp.concatenate(ws[u][SINK:], axis=0)
            atts.append(att_far[:, lanes_of(u)] + dot(vt[at, span_of(u)], w_near, ((1,), (0,))))
        att = jnp.concatenate(atts, axis=1).astype(jnp.bfloat16).astype(jnp.float32)
        delta = jnp.sum(g_all.astype(jnp.float32).T * att, axis=0, keepdims=True)
        ds_far = (jnp.concatenate(ps, axis=1) * (dp_far - delta)).astype(jnp.bfloat16)
        dq_far_ref[0, at] = dot(kt_far[at, :], ds_far, ((1,), (0,)))
        sink_out_ref[0, :, at] += dot(ds_far, q_all, ((1,), (0,))) * SCALE
        sink_out_ref[1, :, at] += dot(w_far, g_all, ((1,), (0,)))
        att_ref[:, 0, :, at] = att.T.astype(jnp.bfloat16).reshape(CHUNKS, ROWS, HD)
        lse_ref[0, h : h + 1, :] = jnp.concatenate(logs, axis=1)
        delta_ref[0, h : h + 1, :] = delta

    @pl.when(step == STEPS - 1)
    def _():
        sink_sent_ref[...] = sink_out_ref[...].astype(jnp.bfloat16)

    kx[:EDGE] = kx[WORK * BLK :]
    vx[:EDGE] = vx[WORK * BLK :]


def backward_kernel(
    lists_ref,
    first_ref,
    kv_ref,
    g_ref,
    lse_ref,
    delta_ref,
    dq_far_ref,
    att_ref,
    prior_ref,
    seg_ref,
    out_ref,
    grads_ref,
    edges_ref,
    prior_out_ref,
    kx,
    vx,
    kt,
    totals,
):
    step = pl.program_id(0)
    run = step // PER_RUN
    local = step % PER_RUN

    @pl.when(local == 0)
    def _():
        totals[:, :EDGE] = jnp.zeros((2, EDGE, COLS), jnp.float32)

    out_ref[:, 0] = att_ref[:, 0]
    window(step, prior_ref, kv_ref, kx, vx)
    masks = masks_of(step, lists_ref, first_ref, seg_ref)
    for h in range(HEADS):
        at = head_of(h)
        kt[at] = kx[:, at].T
        q_all = kv_ref[:, 2, :, at].reshape(WORK * BLK, HD)
        g_all = g_ref[:, 0, :, at].reshape(WORK * BLK, HD)
        lse = lse_ref[0, h : h + 1, :]
        delta = delta_ref[0, h : h + 1, :]
        dq_far = dq_far_ref[0, at]
        qs, gs = blocks(q_all), blocks(g_all)
        ws, dss = [], []
        for u in range(WORK):
            lanes, span = lanes_of(u), span_of(u)
            s = blocks(dot(kx[span, at], qs[u], ((1,), (1,))))
            dp = blocks(dot(vx[span, at], gs[u], ((1,), (1,))))
            near = masks[u][SINK:]
            p = [jnp.exp2(x * (SCALE * LOG2E) + y - lse[:, lanes]) for x, y in zip(s, near)]
            ws.append([x.astype(jnp.bfloat16) for x in p])
            dss.append([(x * (y - delta[:, lanes])).astype(jnp.bfloat16) for x, y in zip(p, dp)])
        dqs = []
        for u in range(WORK):
            ds_near = jnp.concatenate(dss[u], axis=0)
            dqs.append(dq_far[:, lanes_of(u)] + dot(kt[at, span_of(u)], ds_near, ((1,), (0,))))
        dq = (SCALE * jnp.concatenate(dqs, axis=1)).T.astype(jnp.bfloat16)
        out_ref[:, 1, :, at] = dq.reshape(CHUNKS, ROWS, HD)
        for j in range(WORK + REACH):
            used = [u for u in range(WORK) if 0 <= j - u <= REACH]
            lanes = slice(used[0] * BLK, (used[-1] + 1) * BLK)
            ds = jnp.concatenate([dss[u][j - u] for u in used], axis=1)
            w = jnp.concatenate([ws[u][j - u] for u in used], axis=1)
            dk = dot(ds, q_all[lanes], ((1,), (0,))) * SCALE
            dv = dot(w, g_all[lanes], ((1,), (0,)))
            row = slice(j * BLK, (j + 1) * BLK)
            if j < REACH:
                totals[0, row, at] += dk
                totals[1, row, at] += dv
            else:
                totals[0, row, at] = dk
                totals[1, row, at] = dv

    lead = step * CHUNKS
    last = EDGE + BLK
    for n in range(2):
        body = totals[n, EDGE:last].astype(jnp.bfloat16)
        grads_ref[lead, n] = body[:ROWS]
        grads_ref[lead + 1, n, :REST] = body[ROWS:]

        @pl.when(local == 0)
        def _(n=n):
            prior_out_ref[run, n] = totals[n, :EDGE].astype(jnp.bfloat16)

        @pl.when(step == 0)
        def _(n=n):
            edges_ref[n, 0, :BLK] = totals[n, EDGE:last]

        @pl.when(step == 1)
        def _(n=n):
            edges_ref[n, 0, BLK:] = totals[n, :BLK]

        @pl.when(local > 0)
        def _(n=n):
            done = totals[n, :EDGE].astype(jnp.bfloat16)
            grads_ref[lead - 3, n, REST:] = done[:PART]
            grads_ref[lead - 2, n] = done[PART : PART + ROWS]
            grads_ref[lead - 1, n] = done[PART + ROWS :]

        @pl.when(local == PER_RUN - 1)
        def _(n=n):
            tail = totals[n, last:]
            edges_ref[n, 1 + run] = tail
            tail = tail.astype(jnp.bfloat16)
            grads_ref[lead + 1, n, REST:] = tail[:PART]
            grads_ref[lead + 2, n] = tail[PART : PART + ROWS]
            grads_ref[lead + 3, n] = tail[PART + ROWS :]

    kx[:EDGE] = kx[WORK * BLK :]
    vx[:EDGE] = vx[WORK * BLK :]
    totals[:, :EDGE] = totals[:, WORK * BLK :]


LENGTH = EDGE + WORK * BLK
WIDE = pltpu.VMEM((LENGTH, COLS), jnp.bfloat16)
TURNED = pltpu.VMEM((COLS, LENGTH), jnp.bfloat16)
TURNED_FAR = pltpu.VMEM((COLS, EDGE), jnp.bfloat16)
LSE = jax.ShapeDtypeStruct((STEPS, HEADS, WORK * BLK), jnp.float32)
LSE_SPEC = pl.BlockSpec((1, HEADS, WORK * BLK), lambda i, *_: (i, 0, 0))


def whole(x):
    return pl.BlockSpec(x.shape, lambda i, *_: (0,) * len(x.shape))


def moving(count):
    return pl.BlockSpec((CHUNKS, count, ROWS, COLS), lambda i, *_: (i, 0, 0, 0))


DQ_FAR = jax.ShapeDtypeStruct((STEPS, COLS, WORK * BLK), jnp.float32)
DQ_FAR_SPEC = pl.BlockSpec((1, COLS, WORK * BLK), lambda i, *_: (i, 0, 0))


def forward(lists, first, kvq, g, prior, sink_k, sink_v, seg):
    sinks = [
        jax.ShapeDtypeStruct((2, EDGE, COLS), jnp.float32),
        jax.ShapeDtypeStruct((2, EDGE, COLS), jnp.bfloat16),
    ]
    return pl.pallas_call(
        forward_kernel,
        grid_spec=pltpu.PrefetchScalarGridSpec(
            num_scalar_prefetch=2,
            grid=(STEPS,),
            in_specs=[moving(3), moving(1)] + [whole(x) for x in (prior, sink_k, sink_v, seg)],
            out_specs=[moving(1), LSE_SPEC, LSE_SPEC, DQ_FAR_SPEC] + [whole(x) for x in sinks],
            scratch_shapes=[WIDE, WIDE, TURNED, TURNED_FAR, TURNED_FAR],
        ),
        out_shape=[stack_shape(1), LSE, LSE, DQ_FAR] + sinks,
        compiler_params=params(),
        cost_estimate=pl.CostEstimate(flops=6000000000, bytes_accessed=12000000, transcendentals=3000000),
    )(lists, first, kvq, g, prior, sink_k, sink_v, seg)


def backward(lists, first, kvq, g, lse, delta, dq_far, att, prior, seg):
    shapes = [
        stack_shape(2),
        stack_shape(2),
        jax.ShapeDtypeStruct((2, 1 + RUNS, EDGE, COLS), jnp.float32),
        jax.ShapeDtypeStruct((RUNS, 2, EDGE, COLS), jnp.bfloat16),
    ]
    return pl.pallas_call(
        backward_kernel,
        grid_spec=pltpu.PrefetchScalarGridSpec(
            num_scalar_prefetch=2,
            grid=(STEPS,),
            in_specs=[moving(3), moving(1), LSE_SPEC, LSE_SPEC, DQ_FAR_SPEC, moving(1)]
            + [whole(prior), whole(seg)],
            out_specs=[moving(2)] + [whole(x) for x in shapes[1:]],
            scratch_shapes=[WIDE, WIDE, TURNED, pltpu.VMEM((2, LENGTH, COLS), jnp.float32)],
        ),
        out_shape=shapes,
        compiler_params=params(),
        cost_estimate=pl.CostEstimate(flops=6000000000, bytes_accessed=16000000, transcendentals=2000000),
    )(lists, first, kvq, g, lse, delta, dq_far, att, prior, seg)


def put_rows(stage, out_ref, sems, first_chunk, aligned):
    cuts = (0, ROWS, 2 * ROWS, EDGE) if aligned else (0, PART, PART + ROWS, EDGE)
    copies = []
    for n in range(2):
        for i in range(3):
            low, high = cuts[i], cuts[i + 1]
            offset = 0 if aligned or i else REST
            copies.append(
                pltpu.make_async_copy(
                    stage.at[n, pl.ds(low, high - low)],
                    out_ref.at[first_chunk + i, n, pl.ds(offset, high - low)],
                    sems.at[n * 3 + i],
                )
            )
    return copies


def tails_kernel(grads_ref, edges_ref, back_ref, out_ref, stage, sems):
    del grads_ref
    copies = []
    for run in range(RUNS):
        for n in range(2):
            tail = edges_ref[n, 1 + run] + back_ref[run, n].astype(jnp.float32)
            stage[run, n] = tail.astype(jnp.bfloat16)
        first = (run + 1) * RUN_CHUNKS - 3
        copies += put_rows(stage.at[run], out_ref, sems.at[run], first, False)
    for copy in copies:
        copy.start()
    for copy in copies:
        copy.wait()


def head_kernel(owner_ref, grads_ref, edges_ref, total_ref, last_ref, out_ref, stage, sems):
    del grads_ref
    keep = owner_ref[0].astype(jnp.float32)
    for n in range(2):
        add = total_ref[n] + last_ref[n].astype(jnp.float32)
        stage[n] = (edges_ref[n, 0] + add * keep).astype(jnp.bfloat16)
    copies = put_rows(stage, out_ref, sems, 0, True)
    for copy in copies:
        copy.start()
    for copy in copies:
        copy.wait()


ANY = pl.BlockSpec(memory_space=pl.ANY)


def add_tails(grads, edges, back):
    return pl.pallas_call(
        tails_kernel,
        grid=(1,),
        in_specs=[ANY, whole(edges), whole(back)],
        out_specs=ANY,
        out_shape=jax.ShapeDtypeStruct(grads.shape, grads.dtype),
        scratch_shapes=[
            pltpu.VMEM((RUNS, 2, EDGE, COLS), jnp.bfloat16),
            pltpu.SemaphoreType.DMA((RUNS, 6)),
        ],
        input_output_aliases={0: 0},
        compiler_params=params(),
        cost_estimate=pl.CostEstimate(flops=1000000, bytes_accessed=4000000, transcendentals=0),
    )(grads, edges, back)


def add_head(owner, grads, edges, total, last):
    head = pl.BlockSpec((2, 1, EDGE, COLS), lambda i: (0, 0, 0, 0))
    return pl.pallas_call(
        head_kernel,
        grid=(1,),
        in_specs=[pl.BlockSpec(memory_space=pltpu.SMEM), ANY, head] + [whole(x) for x in (total, last)],
        out_specs=ANY,
        out_shape=jax.ShapeDtypeStruct(grads.shape, grads.dtype),
        scratch_shapes=[pltpu.VMEM((2, EDGE, COLS), jnp.bfloat16), pltpu.SemaphoreType.DMA((6,))],
        input_output_aliases={1: 0},
        compiler_params=params(),
        cost_estimate=pl.CostEstimate(flops=1000000, bytes_accessed=3000000, transcendentals=0),
    )(owner, grads, edges, total, last)


def tie_kernel(value_ref, earlier_ref, out_ref):
    del value_ref, earlier_ref, out_ref


def tie(value, earlier):
    spec = pl.BlockSpec(memory_space=pl.ANY)
    return pl.pallas_call(
        tie_kernel,
        in_specs=[spec, spec],
        out_specs=spec,
        out_shape=jax.ShapeDtypeStruct(value.shape, value.dtype),
        input_output_aliases={0: 0},
        compiler_params=params(),
        cost_estimate=pl.CostEstimate(flops=0, bytes_accessed=1024, transcendentals=0),
    )(value, earlier)


def send(value, pairs):
    return lax.ppermute(value, GROUPS, [(a * NZ + b, c * NZ + d) for (a, b), (c, d) in pairs])


EVERY = [(a, b) for a in range(NYO) for b in range(NZ)]
FORWARD = [((a, b), (a, (b + 1) % NZ)) for a, b in EVERY]
BACKWARD = [(b, a) for a, b in FORWARD]
TURN = [((0, NZ - 1), (1, 0))]
TURN_BACK = [((1, 0), (0, NZ - 1))]
ACROSS = [((0, 0), (1, 0))]
EVEN = [[((a, 0), (a, d)) for a in range(NYO)] for d in (2, 4, 6)]
ODD = [((a, b), (a, b + 1)) for a, b in EVERY if b % 2 == 0]
HOPS = [[ACROSS], EVEN, [ODD]]


def spread(value, hop, mine):
    got = functools.reduce(jnp.add, [send(value, pairs) for pairs in hop])
    return jnp.where(mine, value, got)


def collect(total, hop, sent=None):
    sent = total.astype(jnp.bfloat16) if sent is None else sent
    got = [send(sent, [(b, a) for a, b in pairs]) for pairs in hop]
    return functools.reduce(jnp.add, [x.astype(jnp.float32) for x in got], total)


def gathered(value):
    names = ("yi", "c")
    pieces = [value] + [lax.ppermute(value, names, [(i, i ^ d) for i in range(4)]) for d in (1, 2, 3)]
    c_low, yi_low = lax.axis_index("c") == 0, lax.axis_index("yi") == 0
    a, b, c, d = pieces
    a, b, c, d = [jnp.where(c_low, m, n) for m, n in ((a, b), (b, a), (c, d), (d, c))]
    return jnp.concatenate([jnp.where(yi_low, m, n) for m, n in ((a, c), (b, d), (c, a), (d, b))])


def rows_of(both, start, stop, n):
    low, high = start // ROWS, -(-stop // ROWS)
    rows = both[low:high, n].reshape(-1, COLS)
    return rows[start - low * ROWS : stop - low * ROWS]


def per_device(queries, keys, values, grad_out, segment, lists):
    yo, z = lax.axis_index("yo"), lax.axis_index("z")
    small = jnp.concatenate([segment, lists.reshape(-1), jnp.zeros((116,), jnp.int32)])
    small = gathered(small.reshape(1, 512))
    seg = small[:, :384].reshape(BLOCKS, BLK).astype(jnp.float32)
    bounds = small[:, 384:396].reshape(BLOCKS, 4)

    kv = exchange(pack(keys, values, queries))
    sinks = jnp.stack([rows_of(kv, 0, EDGE, n) for n in range(2)])
    sinks = spread(sinks, HOPS[0], yo == 0)
    run_rows = TOK // RUNS
    tails = [[rows_of(kv, r * run_rows - EDGE, r * run_rows, n) for n in range(2)] for r in (1, 2)]
    tails = [jnp.stack(x) for x in tails]
    came = send(jnp.stack(tails), FORWARD)
    turned = send(tails[1], TURN)
    prior = jnp.stack([jnp.where(z == 0, turned, came[0]), jnp.where(z == 0, came[0], came[1])])
    g = exchange(tie(pack(grad_out), prior))
    sinks = spread(sinks, HOPS[1], z == 0)
    sinks = spread(sinks, HOPS[2], z % 2 == 0)

    starts = (jnp.arange(RUNS, dtype=jnp.int32) + yo * RUNS) * NZ + z
    first = starts * (BLOCKS // RUNS)
    att, lse, delta, dq_far, sink_out, sink_sent = forward(
        bounds, first, kv, g, prior, sinks[0], sinks[1], seg
    )
    total = collect(sink_out, HOPS[2], sink_sent)
    out, grads, edges, prior_out = backward(
        bounds, first, kv, g, lse, delta, dq_far, att, prior, seg
    )
    out = exchange(tie(out, total))
    prior_out = tie(prior_out, total)

    went = send(prior_out, BACKWARD)
    turned = send(prior_out[0], TURN_BACK)
    back = jnp.stack([jnp.where(z == NZ - 1, went[1], went[0]), jnp.where(z == NZ - 1, turned, went[1])])
    total = collect(total, HOPS[1])
    last = send(total.astype(jnp.bfloat16), [(b, a) for a, b in ACROSS])

    owner = ((yo == 0) & (z == 0)).astype(jnp.int32).reshape(1)
    grads = add_tails(grads, edges, back)
    grads = exchange(add_head(owner, grads, edges, total, last))
    grad_k, grad_v = unpack(grads)
    attended, grad_q = unpack(out)
    return attended, grad_q, grad_k, grad_v


def solution(mesh):
    fine = Mesh(mesh.devices.reshape(NYO, 2, NZ, 2, 4), ("yo", "yi", "z", "c", "x"))
    ctx = ("yo", "yi", "z", "c")
    rows = P((*ctx, "x"), None)
    return jax.shard_map(
        per_device,
        mesh=fine,
        in_specs=(rows, rows, rows, rows, P(ctx), P(ctx, None, None)),
        out_specs=(rows, rows, rows, rows),
        check_vma=False,
    )
```
